32 devices in a mesh: dp: 4 (over y, x), tensor: 8 (over z, core).
Axes of the slice: x: 2, y: 2, z: 4, core: 2. Of those that a mesh axis runs over, the one named last changes fastest.
Arguments:
- tokens: bfloat16 [1024, 8192], P('dp'), may hold values from -6 to 6
- out_grad: bfloat16 [1024, 8192], P('dp'), may hold values from -6 to 6
- weight_tiles: bfloat16 [256, 2, 3, 128, 128], P(('dp', 'tensor')), may hold values from -0.125 to 0.125
- tile_places: int32 [256, 2], P(('dp', 'tensor')), may hold values from 0 to 1663, as said below
- live_counts: int32 [256], P(('dp', 'tensor')), may hold values from 0 to 2, as said below
Outputs:
- layer_out: bfloat16 [1024, 8192], P('dp', 'tensor')
- input_grad: bfloat16 [1024, 8192], P('dp', 'tensor')
The draws below stay inside these ranges and needn't reach their ends.
Inputs may be any that keep to these rules, and one draw needn't show every extreme that they name: `tile_places`: among the slots addressed to one owner, live or not, no two have the same place; the place 64 * 26 - 1 occurs in a live slot of every owner. `live_counts`: every owner receives 2 live slots from some source, and some owner receives 2 live slots from every source; slots past the count hold padding.
All inputs are finite; a program needn't handle non-finite values.
Results may differ from the reference program's by a relative error of at most 0.012.
Values may be sent and summed in bfloat16 or wider, within the bound.
A program may use at most 192 MiB of HBM per device.

```python
import jax
import jax.numpy as jnp
from jax import lax

D = 8192
TILE = 128
PEER = 2
T_DEV = 256
OWNERS = 8
SOURCES = 32
ROWS = 64
COLS = 26
TOKENS = 1024
N_DP = 4


def slot_plan(key):
    positions = ROWS * COLS
    slot_total = SOURCES * PEER
    perm_key, insert_key, weight_key, count_key, full_key = jax.random.split(jax.random.fold_in(key, 17), 5)
    owner_keys = jax.random.split(perm_key, OWNERS)
    shuffled = jax.vmap(lambda one_key: jax.random.permutation(one_key, positions - 1))(owner_keys)
    forced = jax.random.randint(insert_key, (OWNERS,), 0, SOURCES)
    slot_index = jnp.arange(slot_total)[None, :]
    insert = forced[:, None] * PEER
    source_pos = jnp.where(slot_index < insert, slot_index, slot_index - 1)
    values = jnp.take_along_axis(shuffled, jnp.maximum(source_pos, 0), axis=1)
    values = jnp.where(slot_index == insert, positions - 1, values)
    places = jnp.transpose(values.reshape(OWNERS, SOURCES, PEER), (1, 0, 2)).reshape(SOURCES * OWNERS, PEER)
    owner_weight = jax.random.randint(weight_key, (OWNERS,), 0, 3)
    drawn = jax.random.randint(count_key, (SOURCES, OWNERS), 0, PEER + 1 + owner_weight[None, :])
    drawn = jnp.minimum(drawn, PEER)
    drawn = jnp.where(jnp.arange(SOURCES)[:, None] == forced[None, :], PEER, drawn)
    full_owner = jax.random.randint(full_key, (), 0, OWNERS)
    drawn = jnp.where(jnp.arange(OWNERS)[None, :] == full_owner, PEER, drawn)
    return (places.astype(jnp.int32), drawn.reshape(SOURCES * OWNERS).astype(jnp.int32))


def draw_tile_places(key, part):
    return slot_plan(key)[0]


def draw_live_counts(key, part):
    return slot_plan(key)[1]


def block_scale(rng, dims, shards, least, top_value):
    factor_of, own = 1.0, jax.random.fold_in(rng, 6)
    for axis_at, blocks in shards:
        draws = jnp.exp(jax.random.uniform(jax.random.fold_in(own, axis_at), (blocks,), jnp.float32, least / len(shards), top_value / len(shards)))
        factor_of = factor_of * jnp.repeat(draws, dims[axis_at] // blocks).reshape([-1 if axis == axis_at else 1 for axis in range(len(dims))])
    return factor_of


def centred(own_key, shape, width, limit, shards=(), held_as=jnp.bfloat16):
    values = jax.random.normal(own_key, shape, jnp.float32) * width
    if len(shards) > 0:
        values = block_scale(own_key, shape, shards, -0.22, 0.18) * values
    return jnp.clip(values, min=-limit, max=limit).astype(held_as)


def setup_inputs(seed: int = 0) -> dict:
    seeds = jax.random.split(jax.random.key(seed), 6)
    tokens = centred(seeds[0], (TOKENS, D), 1.0, 6.0, ((0, 4),))
    out_grad = centred(seeds[1], (TOKENS, D), 1.0, 6.0, ((0, 4),))
    weight_tiles = centred(seeds[2], (SOURCES * OWNERS, PEER, 3, TILE, TILE), (D // 4) ** -0.5, 0.125, ((0, 32),))
    tile_places = draw_tile_places(jax.random.fold_in(seeds[5], 71), 0)
    live_counts = draw_live_counts(jax.random.fold_in(seeds[5], 71), 0)
    return dict(tokens=tokens, out_grad=out_grad, weight_tiles=weight_tiles, tile_places=tile_places, live_counts=live_counts)


def owner_pass(token_rows, grad_rows, owner_tiles, owner_places, owner_counts):
    tok_rows = token_rows.shape[0]
    live_mask = (jnp.arange(PEER)[None, :] < owner_counts[:, None]).reshape(-1)
    row_ids = (owner_places // COLS).reshape(-1).astype(jnp.int32)
    col_ids = (owner_places % COLS).reshape(-1).astype(jnp.int32)
    weights = owner_tiles.reshape(SOURCES * PEER, 3, TILE, TILE).astype(jnp.float32)
    weights = weights * live_mask.astype(jnp.float32)[:, None, None, None]
    token_blocks = token_rows.reshape(tok_rows, ROWS, TILE).astype(jnp.float32)
    gathered = jnp.take(token_blocks, row_ids, axis=1)
    products = jnp.einsum("tsa,sgab->sgtb", gathered, weights[:, 0:2])
    preact = jax.ops.segment_sum(products, col_ids, num_segments=COLS)
    gate_pre = jnp.transpose(preact[:, 0], (1, 0, 2))
    up_pre = jnp.transpose(preact[:, 1], (1, 0, 2))
    sigmoid_gate = jax.nn.sigmoid(gate_pre)
    gate_act = gate_pre * sigmoid_gate
    hidden = (gate_act * up_pre).astype(jnp.bfloat16)
    hidden_taken = jnp.take(hidden.astype(jnp.float32), col_ids, axis=1)
    down_prod = jnp.einsum("tsa,sab->stb", hidden_taken, weights[:, 2])
    out_part = jax.ops.segment_sum(down_prod, row_ids, num_segments=ROWS)
    out_part = jnp.transpose(out_part, (1, 0, 2)).reshape(tok_rows, D)
    grad_blocks = grad_rows.reshape(tok_rows, ROWS, TILE).astype(jnp.float32)
    grad_taken = jnp.take(grad_blocks, row_ids, axis=1)
    back_prod = jnp.einsum("tsb,sab->sta", grad_taken, weights[:, 2])
    grad_hidden = jnp.transpose(jax.ops.segment_sum(back_prod, col_ids, num_segments=COLS), (1, 0, 2))
    grad_gate = (grad_hidden * up_pre * (sigmoid_gate * (1.0 + gate_pre * (1.0 - sigmoid_gate)))).astype(jnp.bfloat16)
    grad_up = (grad_hidden * gate_act).astype(jnp.bfloat16)
    grad_pair = jnp.stack([grad_gate, grad_up]).astype(jnp.float32)
    pair_taken = jnp.take(grad_pair, col_ids, axis=2)
    input_prod = jnp.einsum("gtsb,sgab->sta", pair_taken, weights[:, 0:2])
    in_part = jax.ops.segment_sum(input_prod, row_ids, num_segments=ROWS)
    in_part = jnp.transpose(in_part, (1, 0, 2)).reshape(tok_rows, D)
    return out_part.astype(jnp.bfloat16), in_part.astype(jnp.bfloat16)


def reference(tokens, out_grad, weight_tiles, tile_places, live_counts):
    all_tiles = weight_tiles.reshape(SOURCES, OWNERS, PEER, 3, TILE, TILE)
    all_places = tile_places.reshape(SOURCES, OWNERS, PEER)
    all_counts = live_counts.reshape(SOURCES, OWNERS)

    def one_row(row_data):
        token_rows, grad_rows = row_data

        def one_owner(running, owner_index):
            owner_tiles = lax.dynamic_index_in_dim(all_tiles, owner_index, axis=1, keepdims=False)
            owner_places = lax.dynamic_index_in_dim(all_places, owner_index, axis=1, keepdims=False)
            owner_counts = lax.dynamic_index_in_dim(all_counts, owner_index, axis=1, keepdims=False)
            out_part, in_part = owner_pass(token_rows, grad_rows, owner_tiles, owner_places, owner_counts)
            return (running[0] + out_part.astype(jnp.float32), running[1] + in_part.astype(jnp.float32)), None

        zeros_init = jnp.zeros((T_DEV, D), jnp.float32)
        sums, _ = lax.scan(one_owner, (zeros_init, zeros_init), jnp.arange(OWNERS, dtype=jnp.int32))
        return sums[0].astype(jnp.bfloat16), sums[1].astype(jnp.bfloat16)

    layer_out, input_grad = lax.map(one_row, (tokens.reshape(N_DP, T_DEV, D), out_grad.reshape(N_DP, T_DEV, D)))
    return layer_out.reshape(TOKENS, D), input_grad.reshape(TOKENS, D)
```

```python
import functools

import jax
import jax.numpy as jnp
from jax import lax
from jax.experimental import pallas as pl
from jax.experimental.pallas import tpu as pltpu
from jax.sharding import PartitionSpec as P

FF = 26624
GROUP = 8
F32 = jnp.float32
NT = (((1,), (1,)), ((), ()))


def local_kernel(dims, row_ref, col_ref, row_to_ref, col_to_ref, tok_ref, grad_ref, tile_ref, out_ref,
                 pre, back, hid, pair, acc_out, acc_in):
    rows, cols, owners, side, group = dims
    phase, block = pl.program_id(0), pl.program_id(1)
    blocks = pl.num_programs(1)
    per = rows // owners

    @pl.when((phase == 0) & (block == 0))
    def _():
        @pl.loop(0, cols)
        def _(i):
            pre[i] = jnp.zeros(pre.shape[1:], F32)
            back[i] = jnp.zeros(back.shape[1:], F32)

    @pl.when(phase == 0)
    def _():
        for j in range(group):
            s = block * group + j
            at = pl.ds(pl.multiple_of(row_ref[s] * side, side), side)
            to = col_to_ref[s]
            both = jnp.concatenate([tile_ref[j, 0], tile_ref[j, 1]], axis=1)
            pre[to] += jnp.dot(tok_ref[:, at], both, preferred_element_type=F32)
            back[to] += lax.dot_general(grad_ref[:, at], tile_ref[j, 2], NT, preferred_element_type=F32)

    @pl.when((phase == 1) & (block == 0))
    def _():
        @pl.loop(0, cols)
        def _(i):
            gate = pre[i, :, :side]
            up = pre[i, :, side:]
            gh = back[i]
            s = jax.nn.sigmoid(gate)
            act = gate * s
            hid[i] = (act * up).astype(jnp.bfloat16)
            pair[i, :, :side] = (gh * up * (s * (1.0 + gate * (1.0 - s)))).astype(jnp.bfloat16)
            pair[i, :, side:] = (gh * act).astype(jnp.bfloat16)

        @pl.loop(0, rows)
        def _(i):
            acc_out[i] = jnp.zeros(acc_out.shape[1:], F32)
            acc_in[i] = jnp.zeros(acc_in.shape[1:], F32)

    @pl.when(phase == 1)
    def _():
        for j in range(group):
            s = block * group + j
            c = col_ref[s]
            to = row_to_ref[s]
            both = jnp.concatenate([tile_ref[j, 0], tile_ref[j, 1]], axis=1)
            acc_out[to] += jnp.dot(hid[c], tile_ref[j, 2], preferred_element_type=F32)
            acc_in[to] += lax.dot_general(pair[c], both, NT, preferred_element_type=F32)

    @pl.when((phase == 1) & (block == blocks - 1))
    def _():
        @pl.loop(0, owners)
        def _(k):
            for i in range(per):
                out_ref[k, 0, i] = acc_out[k * per + i].astype(jnp.bfloat16)
                out_ref[k, 1, i] = acc_in[k * per + i].astype(jnp.bfloat16)


def local_pass(tokens, out_grad, tiles, row, col, row_to, col_to, owners, cols):
    toks, feats = tokens.shape
    slots, _, side, _ = tiles.shape
    rows = feats // side
    whole = lambda p, b, *_: (0, 0)
    once = pl.Buffered(1)
    return pl.pallas_call(
        functools.partial(local_kernel, (rows, cols, owners, side, GROUP)),
        out_shape=jax.ShapeDtypeStruct((owners, 2, rows // owners, toks, side), jnp.bfloat16),
        grid_spec=pltpu.PrefetchScalarGridSpec(
            num_scalar_prefetch=4,
            grid=(2, slots // GROUP),
            in_specs=[
                pl.BlockSpec((toks, feats), whole, pipeline_mode=once),
                pl.BlockSpec((toks, feats), whole, pipeline_mode=once),
                pl.BlockSpec((GROUP, 3, side, side), lambda p, b, *_: (b, 0, 0, 0)),
            ],
            out_specs=pl.BlockSpec((owners, 2, rows // owners, toks, side), lambda p, b, *_: (0, 0, 0, 0, 0), pipeline_mode=once),
            scratch_shapes=[
                pltpu.VMEM((cols + 1, toks, 2 * side), F32),
                pltpu.VMEM((cols + 1, toks, side), F32),
                pltpu.VMEM((cols, toks, side), jnp.bfloat16),
                pltpu.VMEM((cols, toks, 2 * side), jnp.bfloat16),
                pltpu.VMEM((rows + 1, toks, side), F32),
                pltpu.VMEM((rows + 1, toks, side), F32),
            ],
        ),
        compiler_params=pltpu.CompilerParams(vmem_limit_bytes=58 * 2**20),
        cost_estimate=pl.CostEstimate(flops=12 * slots * toks * side * side, bytes_accessed=30 * 2**20, transcendentals=0),
    )(row, col, row_to, col_to, tokens, out_grad, tiles)


def body(tokens, out_grad, weight_tiles, tile_places, live_counts):
    toks, feats = tokens.shape
    side = weight_tiles.shape[-1]
    peer = weight_tiles.shape[1]
    rows = feats // side
    owners = lax.axis_size("tensor")
    cols = FF // (side * owners)
    meta = jnp.concatenate([tile_places, live_counts[:, None]], axis=1)
    meta = lax.all_gather(meta, ("dp", "tensor"), axis=0)
    mine = lax.dynamic_index_in_dim(meta, lax.axis_index("tensor"), axis=1, keepdims=False)
    places = mine[:, :peer]
    live = (jnp.arange(peer)[None, :] < mine[:, peer:]).reshape(-1)
    row = (places // cols).reshape(-1)
    col = (places % cols).reshape(-1)
    row_to = jnp.where(live, row, rows)
    col_to = jnp.where(live, col, cols)
    tiles = lax.all_to_all(weight_tiles, "tensor", split_axis=0, concat_axis=0, tiled=True)
    tiles = lax.all_gather(tiles, "dp", axis=0, tiled=True)
    tiles = tiles.reshape((-1,) + tiles.shape[2:])
    parts = local_pass(tokens, out_grad, tiles, row, col, row_to, col_to, owners, cols)
    total = lax.psum_scatter(parts, "tensor", scatter_dimension=0, tiled=True)
    total = jnp.transpose(total[0], (0, 2, 1, 3)).reshape(2, toks, feats // owners)
    return total[0], total[1]


def solution(mesh):
    in_specs = (
        P("dp", None),
        P("dp", None),
        P(("dp", "tensor"), None, None, None, None),
        P(("dp", "tensor"), None),
        P(("dp", "tensor")),
    )
    out_specs = (P("dp", "tensor"), P("dp", "tensor"))
    return jax.shard_map(body, mesh=mesh, in_specs=in_specs, out_specs=out_specs, check_vma=False)
```

```python
import functools

import jax
import jax.numpy as jnp
from jax import lax
from jax.experimental import pallas as pl
from jax.experimental.pallas import tpu as pltpu
from jax.sharding import PartitionSpec as P

FF = 26624
GROUP = 8
F32 = jnp.float32
NT = (((1,), (1,)), ((), ()))
MESH = pl.DeviceIdType.MESH
META = 16


def near_first(n):
    order = []
    for o in range(1, n // 2 + 1):
        order += [o] if 2 * o == n else [o, n - o]
    return order


def spread_kernel(n_dp, owners, block_ref, out_ref, own_sem, send_a, recv_a, send_b, recv_b):
    d, t = lax.axis_index("dp"), lax.axis_index("tensor")
    barrier = pltpu.get_barrier_semaphore()
    for o in range(1, owners):
        pl.semaphore_signal(barrier, inc=1, device_id=(d, lax.rem(t + o, owners)), device_id_type=MESH)
    for e in range(1, n_dp):
        pl.semaphore_signal(barrier, inc=1, device_id=(lax.rem(d + e, n_dp), t), device_id_type=MESH)
    pl.semaphore_wait(barrier, owners - 1 + n_dp - 1)

    own = pltpu.make_async_copy(block_ref.at[t], out_ref.at[d, t], own_sem)
    own.start()
    first, second = {}, []

    def forward(src, slot, o):
        for e in range(1, n_dp):
            copy = pltpu.make_async_remote_copy(
                src_ref=src, dst_ref=out_ref.at[d, slot],
                send_sem=send_b.at[e - 1, o], recv_sem=recv_b.at[e - 1, o],
                device_id=(lax.rem(d + e, n_dp), t), device_id_type=MESH)
            copy.start()
            second.append(copy)

    order = near_first(owners)
    for o in order:
        to = lax.rem(t + o, owners)
        first[o] = pltpu.make_async_remote_copy(
            src_ref=block_ref.at[to], dst_ref=out_ref.at[d, t],
            send_sem=send_a.at[o - 1], recv_sem=recv_a.at[o - 1],
            device_id=(d, to), device_id_type=MESH)
        first[o].start()
    forward(block_ref.at[t], t, 0)
    for o in order:
        first[o].wait_recv()
        slot = lax.rem(t + owners - o, owners)
        forward(out_ref.at[d, slot], slot, o)
    own.wait()
    for o in order:
        first[o].wait_send()
    for copy in second:
        copy.wait()


def spread(blocks, n_dp):
    owners, length, side = blocks.shape
    return pl.pallas_call(
        functools.partial(spread_kernel, n_dp, owners),
        out_shape=jax.ShapeDtypeStruct((n_dp, owners, length, side), blocks.dtype),
        in_specs=[pl.BlockSpec(memory_space=pl.ANY)],
        out_specs=pl.BlockSpec(memory_space=pl.ANY),
        scratch_shapes=[
            pltpu.SemaphoreType.DMA(()),
            pltpu.SemaphoreType.DMA((owners - 1,)),
            pltpu.SemaphoreType.DMA((owners - 1,)),
            pltpu.SemaphoreType.DMA((n_dp - 1, owners)),
            pltpu.SemaphoreType.DMA((n_dp - 1, owners)),
        ],
        compiler_params=pltpu.CompilerParams(collective_id=0, has_side_effects=True),
        cost_estimate=pl.CostEstimate(flops=0, bytes_accessed=2 * n_dp * blocks.size * 2, transcendentals=0),
    )(blocks)


def tile_of(tile_ref, peer, j, g):
    side = tile_ref.shape[-1]
    at = (j % peer * 3 + g) * side
    return tile_ref[j // peer, at:at + side]


def local_kernel(dims, row_ref, col_ref, row_to_ref, col_to_ref, tok_ref, grad_ref, tile_ref, out_ref,
                 pre, back, hid, pair, acc_out, acc_in):
    rows, cols, owners, side, peer, group = dims
    phase, block = pl.program_id(0), pl.program_id(1)
    blocks = pl.num_programs(1)
    per = rows // owners

    @pl.when((phase == 0) & (block == 0))
    def _():
        @pl.loop(0, cols)
        def _(i):
            pre[i] = jnp.zeros(pre.shape[1:], F32)
            back[i] = jnp.zeros(back.shape[1:], F32)

    @pl.when(phase == 0)
    def _():
        for j in range(group):
            s = block * group + j
            at = pl.ds(pl.multiple_of(row_ref[s] * side, side), side)
            to = col_to_ref[s]
            both = jnp.concatenate([tile_of(tile_ref, peer, j, 0), tile_of(tile_ref, peer, j, 1)], axis=1)
            pre[to] += jnp.dot(tok_ref[:, at], both, preferred_element_type=F32)
            back[to] += lax.dot_general(grad_ref[:, at], tile_of(tile_ref, peer, j, 2), NT, preferred_element_type=F32)

    @pl.when((phase == 1) & (block == 0))
    def _():
        @pl.loop(0, cols)
        def _(i):
            gate = pre[i, :, :side]
            up = pre[i, :, side:]
            gh = back[i]
            s = jax.nn.sigmoid(gate)
            act = gate * s
            hid[i] = (act * up).astype(jnp.bfloat16)
            pair[i, :, :side] = (gh * up * (s * (1.0 + gate * (1.0 - s)))).astype(jnp.bfloat16)
            pair[i, :, side:] = (gh * act).astype(jnp.bfloat16)

        @pl.loop(0, rows)
        def _(i):
            acc_out[i] = jnp.zeros(acc_out.shape[1:], F32)
            acc_in[i] = jnp.zeros(acc_in.shape[1:], F32)

    @pl.when(phase == 1)
    def _():
        for j in range(group):
            s = block * group + j
            c = col_ref[s]
            to = row_to_ref[s]
            both = jnp.concatenate([tile_of(tile_ref, peer, j, 0), tile_of(tile_ref, peer, j, 1)], axis=1)
            acc_out[to] += jnp.dot(hid[c], tile_of(tile_ref, peer, j, 2), preferred_element_type=F32)
            acc_in[to] += lax.dot_general(pair[c], both, NT, preferred_element_type=F32)

    @pl.when((phase == 1) & (block == blocks - 1))
    def _():
        @pl.loop(0, owners)
        def _(k):
            for i in range(per):
                out_ref[k, 0, i] = acc_out[k * per + i].astype(jnp.bfloat16)
                out_ref[k, 1, i] = acc_in[k * per + i].astype(jnp.bfloat16)


def local_pass(tokens, out_grad, tiles, row, col, row_to, col_to, owners, cols, peer):
    toks, feats = tokens.shape
    sources, length, side = tiles.shape
    slots = sources * peer
    rows = feats // side
    whole = lambda p, b, *_: (0, 0)
    once = pl.Buffered(1)
    return pl.pallas_call(
        functools.partial(local_kernel, (rows, cols, owners, side, peer, GROUP)),
        out_shape=jax.ShapeDtypeStruct((owners, 2, rows // owners, toks, side), jnp.bfloat16),
        grid_spec=pltpu.PrefetchScalarGridSpec(
            num_scalar_prefetch=4,
            grid=(2, slots // GROUP),
            in_specs=[
                pl.BlockSpec((toks, feats), whole, pipeline_mode=once),
                pl.BlockSpec((toks, feats), whole, pipeline_mode=once),
                pl.BlockSpec((GROUP // peer, length, side), lambda p, b, *_: (b, 0, 0)),
            ],
            out_specs=pl.BlockSpec((owners, 2, rows // owners, toks, side), lambda p, b, *_: (0, 0, 0, 0, 0), pipeline_mode=once),
            scratch_shapes=[
                pltpu.VMEM((cols + 1, toks, 2 * side), F32),
                pltpu.VMEM((cols + 1, toks, side), F32),
                pltpu.VMEM((cols, toks, side), jnp.bfloat16),
                pltpu.VMEM((cols, toks, 2 * side), jnp.bfloat16),
                pltpu.VMEM((rows + 1, toks, side), F32),
                pltpu.VMEM((rows + 1, toks, side), F32),
            ],
        ),
        compiler_params=pltpu.CompilerParams(vmem_limit_bytes=58 * 2**20),
        cost_estimate=pl.CostEstimate(flops=12 * slots * toks * side * side, bytes_accessed=30 * 2**20, transcendentals=0),
    )(row, col, row_to, col_to, tokens, out_grad, tiles)


def body(tokens, out_grad, weight_tiles, tile_places, live_counts):
    toks, feats = tokens.shape
    side = weight_tiles.shape[-1]
    peer = weight_tiles.shape[1]
    rows = feats // side
    owners = lax.axis_size("tensor")
    cols = FF // (side * owners)
    n_dp = lax.axis_size("dp")
    live = jnp.arange(peer)[None, :] < live_counts[:, None]
    meta = jnp.concatenate([tile_places // cols, tile_places % cols, live.astype(jnp.int32)], axis=1)
    meta = jnp.pad(meta.astype(jnp.bfloat16), ((0, 0), (0, side - 3 * peer)))
    meta = jnp.broadcast_to(meta[:, None, :], (owners, META, side))
    blocks = jnp.concatenate([weight_tiles.reshape(owners, -1, side), meta], axis=1)
    tiles = spread(blocks, n_dp)
    tiles = tiles.reshape((n_dp * owners,) + tiles.shape[2:])
    meta = tiles[:, -META, :3 * peer].astype(jnp.int32)
    row = meta[:, :peer].reshape(-1)
    col = meta[:, peer:2 * peer].reshape(-1)
    live = meta[:, 2 * peer:].reshape(-1) > 0
    row_to = jnp.where(live, row, rows)
    col_to = jnp.where(live, col, cols)
    parts = local_pass(tokens, out_grad, tiles, row, col, row_to, col_to, owners, cols, peer)
    total = lax.psum_scatter(parts, "tensor", scatter_dimension=0, tiled=True)
    total = jnp.transpose(total[0], (0, 2, 1, 3)).reshape(2, toks, feats // owners)
    return total[0], total[1]


def solution(mesh):
    in_specs = (
        P("dp", None),
        P("dp", None),
        P(("dp", "tensor"), None, None, None, None),
        P(("dp", "tensor"), None),
        P(("dp", "tensor")),
    )
    out_specs = (P("dp", "tensor"), P("dp", "tensor"))
    return jax.shard_map(body, mesh=mesh, in_specs=in_specs, out_specs=out_specs, check_vma=False)
```

```python
import functools

import jax
import jax.numpy as jnp
from jax import lax
from jax.experimental import pallas as pl
from jax.experimental.pallas import tpu as pltpu
from jax.sharding import PartitionSpec as P

FF = 26624
GROUP = 8
F32 = jnp.float32
NT = (((1,), (1,)), ((), ()))
MESH = pl.DeviceIdType.MESH
META = 16


def near_first(n):
    order = []
    for o in range(1, n // 2 + 1):
        order += [o] if 2 * o == n else [o, n - o]
    return order


def spread_kernel(n_dp, owners, block_ref, out_ref, own_sem, send_a, recv_a, send_b, recv_b):
    d, t = lax.axis_index("dp"), lax.axis_index("tensor")
    barrier = pltpu.get_barrier_semaphore()
    for o in range(1, owners):
        pl.semaphore_signal(barrier, inc=1, device_id=(d, lax.rem(t + o, owners)), device_id_type=MESH)
    for e in range(1, n_dp):
        pl.semaphore_signal(barrier, inc=1, device_id=(lax.rem(d + e, n_dp), t), device_id_type=MESH)
    pl.semaphore_wait(barrier, owners - 1 + n_dp - 1)

    own = pltpu.make_async_copy(block_ref.at[t], out_ref.at[d, t], own_sem)
    own.start()
    first, second = {}, []

    def forward(src, slot, o):
        for e in range(1, n_dp):
            copy = pltpu.make_async_remote_copy(
                src_ref=src, dst_ref=out_ref.at[d, slot],
                send_sem=send_b.at[e - 1, o], recv_sem=recv_b.at[e - 1, o],
                device_id=(lax.rem(d + e, n_dp), t), device_id_type=MESH)
            copy.start()
            second.append(copy)

    order = near_first(owners)
    for o in order:
        to = lax.rem(t + o, owners)
        first[o] = pltpu.make_async_remote_copy(
            src_ref=block_ref.at[to], dst_ref=out_ref.at[d, t],
            send_sem=send_a.at[o - 1], recv_sem=recv_a.at[o - 1],
            device_id=(d, to), device_id_type=MESH)
        first[o].start()
    forward(block_ref.at[t], t, 0)
    for o in order:
        first[o].wait_recv()
        slot = lax.rem(t + owners - o, owners)
        forward(out_ref.at[d, slot], slot, o)
    own.wait()
    for o in order:
        first[o].wait_send()
    for copy in second:
        copy.wait()


def square_kernel(n_dp, owners, block_ref, out_ref, own_sem, send_a, recv_a, send_b, recv_b):
    d, t = lax.axis_index("dp"), lax.axis_index("tensor")
    beside = (d + 1 - 2 * lax.rem(d, 2), lax.rem(d + 2, 4))
    barrier = pltpu.get_barrier_semaphore()
    for o in range(1, owners):
        pl.semaphore_signal(barrier, inc=1, device_id=(d, lax.rem(t + o, owners)), device_id_type=MESH)
    for to in beside:
        pl.semaphore_signal(barrier, inc=1, device_id=(to, t), device_id_type=MESH)
    pl.semaphore_wait(barrier, owners - 1 + 2)

    def send(src, row, slot, to, kind, o):
        copy = pltpu.make_async_remote_copy(
            src_ref=src, dst_ref=out_ref.at[row, slot],
            send_sem=send_b.at[kind, o], recv_sem=recv_b.at[kind, o],
            device_id=(to, t), device_id_type=MESH)
        copy.start()
        return copy

    order = near_first(owners)
    first, direct, passed = {}, {}, []

    def outward(src, o):
        slot = lax.rem(t + owners - o, owners)
        direct[o] = [send(src, d, slot, beside[kind], kind, o) for kind in range(2)]

    def onward(i, o):
        slot = lax.rem(t + owners - o, owners)
        via = i % 2
        direct[o][via].wait_recv()
        passed.append(send(out_ref.at[beside[via], slot], beside[via], slot, beside[1 - via], 2, o))

    outward(block_ref.at[t], 0)
    for o in order:
        to = lax.rem(t + o, owners)
        first[o] = pltpu.make_async_remote_copy(
            src_ref=block_ref.at[to], dst_ref=out_ref.at[d, t],
            send_sem=send_a.at[o - 1], recv_sem=recv_a.at[o - 1],
            device_id=(d, to), device_id_type=MESH)
        first[o].start()
    own = pltpu.make_async_copy(block_ref.at[t], out_ref.at[d, t], own_sem)
    own.start()
    turns = [0] + order
    lag = 2
    for i in range(len(turns) + lag):
        if 0 < i < len(turns):
            o = turns[i]
            first[o].wait_recv()
            outward(out_ref.at[d, lax.rem(t + owners - o, owners)], o)
        if i >= lag:
            onward(i - lag, turns[i - lag])
    own.wait()
    for o in order:
        first[o].wait_send()
    for i, o in enumerate(turns):
        direct[o][1 - i % 2].wait_recv()
        direct[o][0].wait_send()
        direct[o][1].wait_send()
    for copy in passed:
        copy.wait()


def spread(blocks, n_dp):
    owners, length, side = blocks.shape
    return pl.pallas_call(
        functools.partial(square_kernel if n_dp == 4 else spread_kernel, n_dp, owners),
        out_shape=jax.ShapeDtypeStruct((n_dp, owners, length, side), blocks.dtype),
        in_specs=[pl.BlockSpec(memory_space=pl.ANY)],
        out_specs=pl.BlockSpec(memory_space=pl.ANY),
        scratch_shapes=[
            pltpu.SemaphoreType.DMA(()),
            pltpu.SemaphoreType.DMA((owners - 1,)),
            pltpu.SemaphoreType.DMA((owners - 1,)),
            pltpu.SemaphoreType.DMA((n_dp - 1, owners)),
            pltpu.SemaphoreType.DMA((n_dp - 1, owners)),
        ],
        compiler_params=pltpu.CompilerParams(collective_id=0, has_side_effects=True),
        cost_estimate=pl.CostEstimate(flops=0, bytes_accessed=2 * n_dp * blocks.size * 2, transcendentals=0),
    )(blocks)


def tile_of(tile_ref, peer, j, g):
    side = tile_ref.shape[-1]
    at = (j % peer * 3 + g) * side
    return tile_ref[j // peer, at:at + side]


def local_kernel(dims, row_ref, col_ref, row_to_ref, col_to_ref, tok_ref, grad_ref, tile_ref, out_ref,
                 pre, back, hid, pair, acc_out, acc_in):
    rows, cols, owners, side, peer, group = dims
    phase, block = pl.program_id(0), pl.program_id(1)
    blocks = pl.num_programs(1)
    per = rows // owners

    @pl.when((phase == 0) & (block == 0))
    def _():
        @pl.loop(0, cols)
        def _(i):
            pre[i] = jnp.zeros(pre.shape[1:], F32)
            back[i] = jnp.zeros(back.shape[1:], F32)

    @pl.when(phase == 0)
    def _():
        for j in range(group):
            s = block * group + j
            at = pl.ds(pl.multiple_of(row_ref[s] * side, side), side)
            to = col_to_ref[s]
            both = jnp.concatenate([tile_of(tile_ref, peer, j, 0), tile_of(tile_ref, peer, j, 1)], axis=1)
            pre[to] += jnp.dot(tok_ref[:, at], both, preferred_element_type=F32)
            back[to] += lax.dot_general(grad_ref[:, at], tile_of(tile_ref, peer, j, 2), NT, preferred_element_type=F32)

    @pl.when((phase == 1) & (block == 0))
    def _():
        @pl.loop(0, cols)
        def _(i):
            gate = pre[i, :, :side]
            up = pre[i, :, side:]
            gh = back[i]
            s = jax.nn.sigmoid(gate)
            act = gate * s
            hid[i] = (act * up).astype(jnp.bfloat16)
            pair[i, :, :side] = (gh * up * (s * (1.0 + gate * (1.0 - s)))).astype(jnp.bfloat16)
            pair[i, :, side:] = (gh * act).astype(jnp.bfloat16)

        @pl.loop(0, rows)
        def _(i):
            acc_out[i] = jnp.zeros(acc_out.shape[1:], F32)
            acc_in[i] = jnp.zeros(acc_in.shape[1:], F32)

    @pl.when(phase == 1)
    def _():
        for j in range(group):
            s = block * group + j
            c = col_ref[s]
            to = row_to_ref[s]
            both = jnp.concatenate([tile_of(tile_ref, peer, j, 0), tile_of(tile_ref, peer, j, 1)], axis=1)
            acc_out[to] += jnp.dot(hid[c], tile_of(tile_ref, peer, j, 2), preferred_element_type=F32)
            acc_in[to] += lax.dot_general(pair[c], both, NT, preferred_element_type=F32)

    @pl.when((phase == 1) & (block == blocks - 1))
    def _():
        @pl.loop(0, owners)
        def _(k):
            for i in range(per):
                out_ref[k, 0, i] = acc_out[k * per + i].astype(jnp.bfloat16)
                out_ref[k, 1, i] = acc_in[k * per + i].astype(jnp.bfloat16)


def local_pass(tokens, out_grad, tiles, row, col, row_to, col_to, owners, cols, peer):
    toks, feats = tokens.shape
    sources, length, side = tiles.shape
    slots = sources * peer
    rows = feats // side
    whole = lambda p, b, *_: (0, 0)
    once = pl.Buffered(1)
    return pl.pallas_call(
        functools.partial(local_kernel, (rows, cols, owners, side, peer, GROUP)),
        out_shape=jax.ShapeDtypeStruct((owners, 2, rows // owners, toks, side), jnp.bfloat16),
        grid_spec=pltpu.PrefetchScalarGridSpec(
            num_scalar_prefetch=4,
            grid=(2, slots // GROUP),
            in_specs=[
                pl.BlockSpec((toks, feats), whole, pipeline_mode=once),
                pl.BlockSpec((toks, feats), whole, pipeline_mode=once),
                pl.BlockSpec((GROUP // peer, length, side), lambda p, b, *_: (b, 0, 0)),
            ],
            out_specs=pl.BlockSpec((owners, 2, rows // owners, toks, side), lambda p, b, *_: (0, 0, 0, 0, 0), pipeline_mode=once),
            scratch_shapes=[
                pltpu.VMEM((cols + 1, toks, 2 * side), F32),
                pltpu.VMEM((cols + 1, toks, side), F32),
                pltpu.VMEM((cols, toks, side), jnp.bfloat16),
                pltpu.VMEM((cols, toks, 2 * side), jnp.bfloat16),
                pltpu.VMEM((rows + 1, toks, side), F32),
                pltpu.VMEM((rows + 1, toks, side), F32),
            ],
        ),
        compiler_params=pltpu.CompilerParams(vmem_limit_bytes=58 * 2**20),
        cost_estimate=pl.CostEstimate(flops=12 * slots * toks * side * side, bytes_accessed=30 * 2**20, transcendentals=0),
    )(row, col, row_to, col_to, tokens, out_grad, tiles)


def body(tokens, out_grad, weight_tiles, tile_places, live_counts):
    toks, feats = tokens.shape
    side = weight_tiles.shape[-1]
    peer = weight_tiles.shape[1]
    rows = feats // side
    owners = lax.axis_size("tensor")
    cols = FF // (side * owners)
    n_dp = lax.axis_size("dp")
    live = jnp.arange(peer)[None, :] < live_counts[:, None]
    meta = jnp.concatenate([tile_places // cols, tile_places % cols, live.astype(jnp.int32)], axis=1)
    meta = jnp.pad(meta.astype(jnp.bfloat16), ((0, 0), (0, side - 3 * peer)))
    meta = jnp.broadcast_to(meta[:, None, :], (owners, META, side))
    blocks = jnp.concatenate([weight_tiles.reshape(owners, -1, side), meta], axis=1)
    tiles = spread(blocks, n_dp)
    tiles = tiles.reshape((n_dp * owners,) + tiles.shape[2:])
    meta = tiles[:, -META, :3 * peer].astype(jnp.int32)
    row = meta[:, :peer].reshape(-1)
    col = meta[:, peer:2 * peer].reshape(-1)
    live = meta[:, 2 * peer:].reshape(-1) > 0
    row_to = jnp.where(live, row, rows)
    col_to = jnp.where(live, col, cols)
    parts = local_pass(tokens, out_grad, tiles, row, col, row_to, col_to, owners, cols, peer)
    total = lax.psum_scatter(parts, "tensor", scatter_dimension=0, tiled=True)
    total = jnp.transpose(total[0], (0, 2, 1, 3)).reshape(2, toks, feats // owners)
    return total[0], total[1]


def solution(mesh):
    in_specs = (
        P("dp", None),
        P("dp", None),
        P(("dp", "tensor"), None, None, None, None),
        P(("dp", "tensor"), None),
        P(("dp", "tensor")),
    )
    out_specs = (P("dp", "tensor"), P("dp", "tensor"))
    return jax.shard_map(body, mesh=mesh, in_specs=in_specs, out_specs=out_specs, check_vma=False)
```

```python
import functools

import jax
import jax.numpy as jnp
from jax import lax
from jax.experimental import pallas as pl
from jax.experimental.pallas import tpu as pltpu
from jax.sharding import PartitionSpec as P

FF = 26624
GROUP = 8
F32 = jnp.float32
NT = (((1,), (1,)), ((), ()))
MESH = pl.DeviceIdType.MESH
META = 16


def near_first(n):
    order = []
    for o in range(1, n // 2 + 1):
        order += [o] if 2 * o == n else [o, n - o]
    return order


def spread_kernel(n_dp, owners, block_ref, out_ref, own_sem, send_a, recv_a, send_b, recv_b):
    d, t = lax.axis_index("dp"), lax.axis_index("tensor")
    barrier = pltpu.get_barrier_semaphore()
    for o in range(1, owners):
        pl.semaphore_signal(barrier, inc=1, device_id=(d, lax.rem(t + o, owners)), device_id_type=MESH)
    for e in range(1, n_dp):
        pl.semaphore_signal(barrier, inc=1, device_id=(lax.rem(d + e, n_dp), t), device_id_type=MESH)
    pl.semaphore_wait(barrier, owners - 1 + n_dp - 1)

    own = pltpu.make_async_copy(block_ref.at[t], out_ref.at[d, t], own_sem)
    own.start()
    first, second = {}, []

    def forward(src, slot, o):
        for e in range(1, n_dp):
            copy = pltpu.make_async_remote_copy(
                src_ref=src, dst_ref=out_ref.at[d, slot],
                send_sem=send_b.at[e - 1, o], recv_sem=recv_b.at[e - 1, o],
                device_id=(lax.rem(d + e, n_dp), t), device_id_type=MESH)
            copy.start()
            second.append(copy)

    order = near_first(owners)
    for o in order:
        to = lax.rem(t + o, owners)
        first[o] = pltpu.make_async_remote_copy(
            src_ref=block_ref.at[to], dst_ref=out_ref.at[d, t],
            send_sem=send_a.at[o - 1], recv_sem=recv_a.at[o - 1],
            device_id=(d, to), device_id_type=MESH)
        first[o].start()
    forward(block_ref.at[t], t, 0)
    for o in order:
        first[o].wait_recv()
        slot = lax.rem(t + owners - o, owners)
        forward(out_ref.at[d, slot], slot, o)
    own.wait()
    for o in order:
        first[o].wait_send()
    for copy in second:
        copy.wait()


def square_kernel(n_dp, owners, block_ref, out_ref, own_sem, send_a, recv_a, send_b, recv_b):
    d, t = lax.axis_index("dp"), lax.axis_index("tensor")
    beside = (d + 1 - 2 * lax.rem(d, 2), lax.rem(d + 2, 4))
    barrier = pltpu.get_barrier_semaphore()
    for o in range(1, owners):
        pl.semaphore_signal(barrier, inc=1, device_id=(d, lax.rem(t + o, owners)), device_id_type=MESH)
    for to in beside:
        pl.semaphore_signal(barrier, inc=1, device_id=(to, t), device_id_type=MESH)
    pl.semaphore_wait(barrier, owners - 1 + 2)

    def send(src, row, slot, to, kind, o):
        copy = pltpu.make_async_remote_copy(
            src_ref=src, dst_ref=out_ref.at[row, slot],
            send_sem=send_b.at[kind, o], recv_sem=recv_b.at[kind, o],
            device_id=(to, t), device_id_type=MESH)
        copy.start()
        return copy

    order = near_first(owners)
    first, direct, passed = {}, {}, []

    def outward(src, o):
        slot = lax.rem(t + owners - o, owners)
        direct[o] = [send(src, d, slot, beside[kind], kind, o) for kind in range(2)]

    def onward(i, o):
        slot = lax.rem(t + owners - o, owners)
        via = i % 2
        direct[o][via].wait_recv()
        passed.append(send(out_ref.at[beside[via], slot], beside[via], slot, beside[1 - via], 2, o))

    outward(block_ref.at[t], 0)
    for o in order:
        to = lax.rem(t + o, owners)
        first[o] = pltpu.make_async_remote_copy(
            src_ref=block_ref.at[to], dst_ref=out_ref.at[d, t],
            send_sem=send_a.at[o - 1], recv_sem=recv_a.at[o - 1],
            device_id=(d, to), device_id_type=MESH)
        first[o].start()
    own = pltpu.make_async_copy(block_ref.at[t], out_ref.at[d, t], own_sem)
    own.start()
    turns = [0] + order
    lag = 2
    for i in range(len(turns) + lag):
        if 0 < i < len(turns):
            o = turns[i]
            first[o].wait_recv()
            outward(out_ref.at[d, lax.rem(t + owners - o, owners)], o)
        if i >= lag:
            onward(i - lag, turns[i - lag])
    own.wait()
    for o in order:
        first[o].wait_send()
    for i, o in enumerate(turns):
        direct[o][1 - i % 2].wait_recv()
        direct[o][0].wait_send()
        direct[o][1].wait_send()
    for copy in passed:
        copy.wait()


def spread(blocks, n_dp):
    owners, length, side = blocks.shape
    return pl.pallas_call(
        functools.partial(square_kernel if n_dp == 4 else spread_kernel, n_dp, owners),
        out_shape=jax.ShapeDtypeStruct((n_dp, owners, length, side), blocks.dtype),
        in_specs=[pl.BlockSpec(memory_space=pl.ANY)],
        out_specs=pl.BlockSpec(memory_space=pl.ANY),
        scratch_shapes=[
            pltpu.SemaphoreType.DMA(()),
            pltpu.SemaphoreType.DMA((owners - 1,)),
            pltpu.SemaphoreType.DMA((owners - 1,)),
            pltpu.SemaphoreType.DMA((n_dp - 1, owners)),
            pltpu.SemaphoreType.DMA((n_dp - 1, owners)),
        ],
        compiler_params=pltpu.CompilerParams(collective_id=0, has_side_effects=True),
        cost_estimate=pl.CostEstimate(flops=0, bytes_accessed=2 * n_dp * blocks.size * 2, transcendentals=0),
    )(blocks)


def line_kernel(chips, chunks, part_ref, out_ref, in_ref, mate_buf, sent, from_buf,
                mate_send, mate_recv, line_send, line_recv):
    d, t = lax.axis_index("dp"), lax.axis_index("tensor")
    z, c = t // 2, lax.rem(t, 2)
    owners, last = 2 * chips, chips - 1
    mate = t + 1 - 2 * c
    tiles = part_ref.shape[1]
    size = tiles // chunks
    half = tiles // 2
    side = part_ref.shape[-1]
    onward = (lax.rem(t + 2, owners), lax.rem(t + owners - 2, owners))
    has_next = (z < last, z > 0)
    has_before = (z > 0, z < last)

    barrier = pltpu.get_barrier_semaphore()
    pl.semaphore_signal(barrier, inc=1, device_id=(d, mate), device_id_type=MESH)
    for way in range(2):
        @pl.when(has_next[way])
        def _():
            pl.semaphore_signal(barrier, inc=1, device_id=(d, onward[way]), device_id_type=MESH)
    inner = (z > 0) & (z < last)

    @pl.when(inner)
    def _():
        pl.semaphore_wait(barrier, 3)

    @pl.when(jnp.logical_not(inner))
    def _():
        pl.semaphore_wait(barrier, 2)

    swaps = {}
    order = []
    for k in range(chips // 2):
        order += [last - k, k]
    for to in order:
        swaps[to] = pltpu.make_async_remote_copy(
            src_ref=part_ref.at[2 * to + 1 - c], dst_ref=mate_buf.at[to],
            send_sem=mate_send.at[to], recv_sem=mate_recv.at[to],
            device_id=(d, mate), device_id_type=MESH)
        swaps[to].start()
    for to in order:
        swaps[to].wait_recv()

    def hop(way, to, q):
        at = pl.ds(q * size, size)
        return pltpu.make_async_remote_copy(
            src_ref=sent.at[to, at], dst_ref=from_buf.at[way, to, at],
            send_sem=line_send.at[way, to, q], recv_sem=line_recv.at[way, to, q],
            device_id=(d, onward[way]), device_id_type=MESH)

    def own_sum(to, i):
        return part_ref[2 * to + c, i].astype(F32) + mate_buf[to, i].astype(F32)

    for k in range(last):
        @pl.loop(0, chunks)
        def _(q):
            for way, to in ((0, last - k), (1, k)):
                goes = (z < to) if way == 0 else (z > to)

                @pl.when(goes & has_before[way])
                def _():
                    hop(way, to, q).wait_recv()
                    for j in range(size):
                        i = q * size + j
                        sent[to, i] = (own_sum(to, i) + from_buf[way, to, i].astype(F32)).astype(jnp.bfloat16)
                    hop(way, to, q).start()

                @pl.when(goes & jnp.logical_not(has_before[way]))
                def _():
                    for j in range(size):
                        i = q * size + j
                        sent[to, i] = own_sum(to, i).astype(jnp.bfloat16)
                    hop(way, to, q).start()

    def finish(ways):
        for q in range(chunks):
            for way in ways:
                hop(way, z, q).wait_recv()
            for j in range(size):
                i = q * size + j
                total = own_sum(z, i)
                for way in ways:
                    total = total + from_buf[way, z, i].astype(F32)
                to_ref = out_ref if i < half else in_ref
                col = i % half * side
                to_ref[:, col:col + side] = total.astype(jnp.bfloat16)

    @pl.when(z == 0)
    def _():
        finish((1,))

    @pl.when(z == last)
    def _():
        finish((0,))

    @pl.when((z > 0) & (z < last))
    def _():
        finish((0, 1))

    for to in order:
        swaps[to].wait_send()
    for k in range(last):
        @pl.loop(0, chunks)
        def _(q):
            for way, to in ((0, last - k), (1, k)):
                goes = (z < to) if way == 0 else (z > to)

                @pl.when(goes)
                def _():
                    hop(way, to, q).wait_send()


def line_sum(parts, chunks=4):
    owners, _, per, toks, side = parts.shape
    chips, tiles = owners // 2, 2 * per
    parts = parts.reshape(owners, tiles, toks, side)
    result = jax.ShapeDtypeStruct((toks, per * side), jnp.bfloat16)
    vmem = pl.BlockSpec(memory_space=pltpu.VMEM)
    return pl.pallas_call(
        functools.partial(line_kernel, chips, chunks),
        out_shape=(result, result),
        in_specs=[vmem],
        out_specs=(vmem, vmem),
        scratch_shapes=[
            pltpu.VMEM((chips, tiles, toks, side), jnp.bfloat16),
            pltpu.VMEM((chips, tiles, toks, side), jnp.bfloat16),
            pltpu.VMEM((2, chips, tiles, toks, side), jnp.bfloat16),
            pltpu.SemaphoreType.DMA((chips,)),
            pltpu.SemaphoreType.DMA((chips,)),
            pltpu.SemaphoreType.DMA((2, chips, chunks)),
            pltpu.SemaphoreType.DMA((2, chips, chunks)),
        ],
        compiler_params=pltpu.CompilerParams(collective_id=1, has_side_effects=True, vmem_limit_bytes=48 * 2**20),
        cost_estimate=pl.CostEstimate(flops=parts.size, bytes_accessed=2 * parts.size, transcendentals=0),
    )(parts)


def tile_of(tile_ref, peer, j, g):
    side = tile_ref.shape[-1]
    at = (j % peer * 3 + g) * side
    return tile_ref[j // peer, at:at + side]


def local_kernel(dims, row_ref, col_ref, row_to_ref, col_to_ref, tok_ref, grad_ref, tile_ref, out_ref,
                 pre, back, hid, pair, acc_out, acc_in):
    rows, cols, owners, side, peer, group = dims
    phase, block = pl.program_id(0), pl.program_id(1)
    blocks = pl.num_programs(1)
    per = rows // owners

    @pl.when((phase == 0) & (block == 0))
    def _():
        @pl.loop(0, cols)
        def _(i):
            pre[i] = jnp.zeros(pre.shape[1:], F32)
            back[i] = jnp.zeros(back.shape[1:], F32)

    @pl.when(phase == 0)
    def _():
        for j in range(group):
            s = block * group + j
            at = pl.ds(pl.multiple_of(row_ref[s] * side, side), side)
            to = col_to_ref[s]
            both = jnp.concatenate([tile_of(tile_ref, peer, j, 0), tile_of(tile_ref, peer, j, 1)], axis=1)
            pre[to] += jnp.dot(tok_ref[:, at], both, preferred_element_type=F32)
            back[to] += lax.dot_general(grad_ref[:, at], tile_of(tile_ref, peer, j, 2), NT, preferred_element_type=F32)

    @pl.when((phase == 1) & (block == 0))
    def _():
        @pl.loop(0, cols)
        def _(i):
            gate = pre[i, :, :side]
            up = pre[i, :, side:]
            gh = back[i]
            s = jax.nn.sigmoid(gate)
            act = gate * s
            hid[i] = (act * up).astype(jnp.bfloat16)
            pair[i, :, :side] = (gh * up * (s * (1.0 + gate * (1.0 - s)))).astype(jnp.bfloat16)
            pair[i, :, side:] = (gh * act).astype(jnp.bfloat16)

        @pl.loop(0, rows)
        def _(i):
            acc_out[i] = jnp.zeros(acc_out.shape[1:], F32)
            acc_in[i] = jnp.zeros(acc_in.shape[1:], F32)

    @pl.when(phase == 1)
    def _():
        for j in range(group):
            s = block * group + j
            c = col_ref[s]
            to = row_to_ref[s]
            both = jnp.concatenate([tile_of(tile_ref, peer, j, 0), tile_of(tile_ref, peer, j, 1)], axis=1)
            acc_out[to] += jnp.dot(hid[c], tile_of(tile_ref, peer, j, 2), preferred_element_type=F32)
            acc_in[to] += lax.dot_general(pair[c], both, NT, preferred_element_type=F32)

    @pl.when((phase == 1) & (block == blocks - 1))
    def _():
        @pl.loop(0, owners)
        def _(k):
            for i in range(per):
                out_ref[k, 0, i] = acc_out[k * per + i].astype(jnp.bfloat16)
                out_ref[k, 1, i] = acc_in[k * per + i].astype(jnp.bfloat16)


def local_pass(tokens, out_grad, tiles, row, col, row_to, col_to, owners, cols, peer):
    toks, feats = tokens.shape
    sources, length, side = tiles.shape
    slots = sources * peer
    rows = feats // side
    whole = lambda p, b, *_: (0, 0)
    once = pl.Buffered(1)
    return pl.pallas_call(
        functools.partial(local_kernel, (rows, cols, owners, side, peer, GROUP)),
        out_shape=jax.ShapeDtypeStruct((owners, 2, rows // owners, toks, side), jnp.bfloat16),
        grid_spec=pltpu.PrefetchScalarGridSpec(
            num_scalar_prefetch=4,
            grid=(2, slots // GROUP),
            in_specs=[
                pl.BlockSpec((toks, feats), whole, pipeline_mode=once),
                pl.BlockSpec((toks, feats), whole, pipeline_mode=once),
                pl.BlockSpec((GROUP // peer, length, side), lambda p, b, *_: (b, 0, 0)),
            ],
            out_specs=pl.BlockSpec((owners, 2, rows // owners, toks, side), lambda p, b, *_: (0, 0, 0, 0, 0), pipeline_mode=once),
            scratch_shapes=[
                pltpu.VMEM((cols + 1, toks, 2 * side), F32),
                pltpu.VMEM((cols + 1, toks, side), F32),
                pltpu.VMEM((cols, toks, side), jnp.bfloat16),
                pltpu.VMEM((cols, toks, 2 * side), jnp.bfloat16),
                pltpu.VMEM((rows + 1, toks, side), F32),
                pltpu.VMEM((rows + 1, toks, side), F32),
            ],
        ),
        compiler_params=pltpu.CompilerParams(vmem_limit_bytes=58 * 2**20),
        cost_estimate=pl.CostEstimate(flops=12 * slots * toks * side * side, bytes_accessed=30 * 2**20, transcendentals=0),
    )(row, col, row_to, col_to, tokens, out_grad, tiles)


def body(tokens, out_grad, weight_tiles, tile_places, live_counts):
    toks, feats = tokens.shape
    side = weight_tiles.shape[-1]
    peer = weight_tiles.shape[1]
    rows = feats // side
    owners = lax.axis_size("tensor")
    cols = FF // (side * owners)
    n_dp = lax.axis_size("dp")
    live = jnp.arange(peer)[None, :] < live_counts[:, None]
    meta = jnp.concatenate([tile_places // cols, tile_places % cols, live.astype(jnp.int32)], axis=1)
    meta = jnp.pad(meta.astype(jnp.bfloat16), ((0, 0), (0, side - 3 * peer)))
    meta = jnp.broadcast_to(meta[:, None, :], (owners, META, side))
    blocks = jnp.concatenate([weight_tiles.reshape(owners, -1, side), meta], axis=1)
    tiles = spread(blocks, n_dp)
    tiles = tiles.reshape((n_dp * owners,) + tiles.shape[2:])
    meta = tiles[:, -META, :3 * peer].astype(jnp.int32)
    row = meta[:, :peer].reshape(-1)
    col = meta[:, peer:2 * peer].reshape(-1)
    live = meta[:, 2 * peer:].reshape(-1) > 0
    row_to = jnp.where(live, row, rows)
    col_to = jnp.where(live, col, cols)
    parts = local_pass(tokens, out_grad, tiles, row, col, row_to, col_to, owners, cols, peer)
    if (n_dp, owners) == (4, 8):
        return line_sum(parts)
    total = lax.psum_scatter(parts, "tensor", scatter_dimension=0, tiled=True)
    total = jnp.transpose(total[0], (0, 2, 1, 3)).reshape(2, toks, feats // owners)
    return total[0], total[1]


def solution(mesh):
    in_specs = (
        P("dp", None),
        P("dp", None),
        P(("dp", "tensor"), None, None, None, None),
        P(("dp", "tensor"), None),
        P(("dp", "tensor")),
    )
    out_specs = (P("dp", "tensor"), P("dp", "tensor"))
    return jax.shard_map(body, mesh=mesh, in_specs=in_specs, out_specs=out_specs, check_vma=False)
```

```python
import functools

import jax
import jax.numpy as jnp
from jax import lax
from jax.experimental import pallas as pl
from jax.experimental.pallas import tpu as pltpu
from jax.sharding import PartitionSpec as P

FF = 26624
GROUP = 8
F32 = jnp.float32
NT = (((1,), (1,)), ((), ()))
MESH = pl.DeviceIdType.MESH
META = 16


def near_first(n):
    order = []
    for o in range(1, n // 2 + 1):
        order += [o] if 2 * o == n else [o, n - o]
    return order


def spread_kernel(n_dp, owners, block_ref, out_ref, own_sem, send_a, recv_a, send_b, recv_b):
    d, t = lax.axis_index("dp"), lax.axis_index("tensor")
    barrier = pltpu.get_barrier_semaphore()
    for o in range(1, owners):
        pl.semaphore_signal(barrier, inc=1, device_id=(d, lax.rem(t + o, owners)), device_id_type=MESH)
    for e in range(1, n_dp):
        pl.semaphore_signal(barrier, inc=1, device_id=(lax.rem(d + e, n_dp), t), device_id_type=MESH)
    pl.semaphore_wait(barrier, owners - 1 + n_dp - 1)

    own = pltpu.make_async_copy(block_ref.at[t], out_ref.at[d, t], own_sem)
    own.start()
    first, second = {}, []

    def forward(src, slot, o):
        for e in range(1, n_dp):
            copy = pltpu.make_async_remote_copy(
                src_ref=src, dst_ref=out_ref.at[d, slot],
                send_sem=send_b.at[e - 1, o], recv_sem=recv_b.at[e - 1, o],
                device_id=(lax.rem(d + e, n_dp), t), device_id_type=MESH)
            copy.start()
            second.append(copy)

    order = near_first(owners)
    for o in order:
        to = lax.rem(t + o, owners)
        first[o] = pltpu.make_async_remote_copy(
            src_ref=block_ref.at[to], dst_ref=out_ref.at[d, t],
            send_sem=send_a.at[o - 1], recv_sem=recv_a.at[o - 1],
            device_id=(d, to), device_id_type=MESH)
        first[o].start()
    forward(block_ref.at[t], t, 0)
    for o in order:
        first[o].wait_recv()
        slot = lax.rem(t + owners - o, owners)
        forward(out_ref.at[d, slot], slot, o)
    own.wait()
    for o in order:
        first[o].wait_send()
    for copy in second:
        copy.wait()


def square_kernel(n_dp, owners, block_ref, out_ref, own_sem, send_a, recv_a, send_b, recv_b):
    d, t = lax.axis_index("dp"), lax.axis_index("tensor")
    beside = (d + 1 - 2 * lax.rem(d, 2), lax.rem(d + 2, 4))
    barrier = pltpu.get_barrier_semaphore()
    for o in range(1, owners):
        pl.semaphore_signal(barrier, inc=1, device_id=(d, lax.rem(t + o, owners)), device_id_type=MESH)
    for to in beside:
        pl.semaphore_signal(barrier, inc=1, device_id=(to, t), device_id_type=MESH)
    pl.semaphore_wait(barrier, owners - 1 + 2)

    def send(src, row, slot, to, kind, o):
        copy = pltpu.make_async_remote_copy(
            src_ref=src, dst_ref=out_ref.at[row, slot],
            send_sem=send_b.at[kind, o], recv_sem=recv_b.at[kind, o],
            device_id=(to, t), device_id_type=MESH)
        copy.start()
        return copy

    order = near_first(owners)
    first, direct, passed = {}, {}, []

    def outward(src, o):
        slot = lax.rem(t + owners - o, owners)
        direct[o] = [send(src, d, slot, beside[kind], kind, o) for kind in range(2)]

    def onward(i, o):
        slot = lax.rem(t + owners - o, owners)
        via = i % 2
        direct[o][via].wait_recv()
        passed.append(send(out_ref.at[beside[via], slot], beside[via], slot, beside[1 - via], 2, o))

    outward(block_ref.at[t], 0)
    for o in order:
        to = lax.rem(t + o, owners)
        first[o] = pltpu.make_async_remote_copy(
            src_ref=block_ref.at[to], dst_ref=out_ref.at[d, t],
            send_sem=send_a.at[o - 1], recv_sem=recv_a.at[o - 1],
            device_id=(d, to), device_id_type=MESH)
        first[o].start()
    own = pltpu.make_async_copy(block_ref.at[t], out_ref.at[d, t], own_sem)
    own.start()
    turns = [0] + order
    lag = 2
    for i in range(len(turns) + lag):
        if 0 < i < len(turns):
            o = turns[i]
            first[o].wait_recv()
            outward(out_ref.at[d, lax.rem(t + owners - o, owners)], o)
        if i >= lag:
            onward(i - lag, turns[i - lag])
    own.wait()
    for o in order:
        first[o].wait_send()
    for i, o in enumerate(turns):
        direct[o][1 - i % 2].wait_recv()
        direct[o][0].wait_send()
        direct[o][1].wait_send()
    for copy in passed:
        copy.wait()


def spread(blocks, n_dp):
    owners, length, side = blocks.shape
    return pl.pallas_call(
        functools.partial(square_kernel if n_dp == 4 else spread_kernel, n_dp, owners),
        out_shape=jax.ShapeDtypeStruct((n_dp, owners, length, side), blocks.dtype),
        in_specs=[pl.BlockSpec(memory_space=pl.ANY)],
        out_specs=pl.BlockSpec(memory_space=pl.ANY),
        scratch_shapes=[
            pltpu.SemaphoreType.DMA(()),
            pltpu.SemaphoreType.DMA((owners - 1,)),
            pltpu.SemaphoreType.DMA((owners - 1,)),
            pltpu.SemaphoreType.DMA((n_dp - 1, owners)),
            pltpu.SemaphoreType.DMA((n_dp - 1, owners)),
        ],
        compiler_params=pltpu.CompilerParams(collective_id=0, has_side_effects=True),
        cost_estimate=pl.CostEstimate(flops=0, bytes_accessed=2 * n_dp * blocks.size * 2, transcendentals=0),
    )(blocks)


def line_kernel(chips, chunks, part_ref, out_ref, in_ref, own_buf, mate_buf, sent, from_buf,
                own_sem, mate_send, mate_recv, line_send, line_recv):
    d, t = lax.axis_index("dp"), lax.axis_index("tensor")
    z, c = t // 2, lax.rem(t, 2)
    owners, last = 2 * chips, chips - 1
    mate = t + 1 - 2 * c
    tiles = part_ref.shape[1]
    size = tiles // chunks
    half = tiles // 2
    side = part_ref.shape[-1]
    onward = (lax.rem(t + 2, owners), lax.rem(t + owners - 2, owners))
    has_next = (z < last, z > 0)
    has_before = (z > 0, z < last)

    barrier = pltpu.get_barrier_semaphore()
    pl.semaphore_signal(barrier, inc=1, device_id=(d, mate), device_id_type=MESH)
    for way in range(2):
        @pl.when(has_next[way])
        def _():
            pl.semaphore_signal(barrier, inc=1, device_id=(d, onward[way]), device_id_type=MESH)
    inner = (z > 0) & (z < last)

    @pl.when(inner)
    def _():
        pl.semaphore_wait(barrier, 3)

    @pl.when(jnp.logical_not(inner))
    def _():
        pl.semaphore_wait(barrier, 2)

    swaps, loads = {}, {}
    order = []
    for k in range(chips // 2):
        order += [last - k, k]
    for to in order:
        swaps[to] = pltpu.make_async_remote_copy(
            src_ref=part_ref.at[2 * to + 1 - c], dst_ref=mate_buf.at[to],
            send_sem=mate_send.at[to], recv_sem=mate_recv.at[to],
            device_id=(d, mate), device_id_type=MESH)
        swaps[to].start()
        loads[to] = pltpu.make_async_copy(part_ref.at[2 * to + c], own_buf.at[to], own_sem.at[to])
        loads[to].start()

    def hop(way, to, q):
        at = pl.ds(q * size, size)
        return pltpu.make_async_remote_copy(
            src_ref=sent.at[to, at], dst_ref=from_buf.at[way, to, at],
            send_sem=line_send.at[way, to, q], recv_sem=line_recv.at[way, to, q],
            device_id=(d, onward[way]), device_id_type=MESH)

    def own_sum(to, i):
        return own_buf[to, i].astype(F32) + mate_buf[to, i].astype(F32)

    for k in range(last):
        for to in order[2 * k:2 * k + 2]:
            loads[to].wait()
            swaps[to].wait_recv()

        @pl.loop(0, chunks)
        def _(q):
            for way, to in ((0, last - k), (1, k)):
                goes = (z < to) if way == 0 else (z > to)

                @pl.when(goes & has_before[way])
                def _():
                    hop(way, to, q).wait_recv()
                    for j in range(size):
                        i = q * size + j
                        sent[to, i] = (own_sum(to, i) + from_buf[way, to, i].astype(F32)).astype(jnp.bfloat16)
                    hop(way, to, q).start()

                @pl.when(goes & jnp.logical_not(has_before[way]))
                def _():
                    for j in range(size):
                        i = q * size + j
                        sent[to, i] = own_sum(to, i).astype(jnp.bfloat16)
                    hop(way, to, q).start()

    def finish(ways):
        for q in range(chunks):
            for way in ways:
                hop(way, z, q).wait_recv()
            for j in range(size):
                i = q * size + j
                total = own_sum(z, i)
                for way in ways:
                    total = total + from_buf[way, z, i].astype(F32)
                to_ref = out_ref if i < half else in_ref
                col = i % half * side
                to_ref[:, col:col + side] = total.astype(jnp.bfloat16)

    @pl.when(z == 0)
    def _():
        finish((1,))

    @pl.when(z == last)
    def _():
        finish((0,))

    @pl.when((z > 0) & (z < last))
    def _():
        finish((0, 1))

    for to in order:
        swaps[to].wait_send()
    for k in range(last):
        @pl.loop(0, chunks)
        def _(q):
            for way, to in ((0, last - k), (1, k)):
                goes = (z < to) if way == 0 else (z > to)

                @pl.when(goes)
                def _():
                    hop(way, to, q).wait_send()


def line_sum(parts, chunks=4):
    owners, _, per, toks, side = parts.shape
    chips, tiles = owners // 2, 2 * per
    parts = parts.reshape(owners, tiles, toks, side)
    result = jax.ShapeDtypeStruct((toks, per * side), jnp.bfloat16)
    vmem = pl.BlockSpec(memory_space=pltpu.VMEM)
    return pl.pallas_call(
        functools.partial(line_kernel, chips, chunks),
        out_shape=(result, result),
        in_specs=[pl.BlockSpec(memory_space=pl.ANY)],
        out_specs=(vmem, vmem),
        scratch_shapes=[
            pltpu.VMEM((chips, tiles, toks, side), jnp.bfloat16),
            pltpu.VMEM((chips, tiles, toks, side), jnp.bfloat16),
            pltpu.VMEM((chips, tiles, toks, side), jnp.bfloat16),
            pltpu.VMEM((2, chips, tiles, toks, side), jnp.bfloat16),
            pltpu.SemaphoreType.DMA((chips,)),
            pltpu.SemaphoreType.DMA((chips,)),
            pltpu.SemaphoreType.DMA((chips,)),
            pltpu.SemaphoreType.DMA((2, chips, chunks)),
            pltpu.SemaphoreType.DMA((2, chips, chunks)),
        ],
        compiler_params=pltpu.CompilerParams(collective_id=1, has_side_effects=True, vmem_limit_bytes=58 * 2**20),
        cost_estimate=pl.CostEstimate(flops=parts.size, bytes_accessed=2 * parts.size, transcendentals=0),
    )(parts)


def tile_of(tile_ref, peer, j, g):
    side = tile_ref.shape[-1]
    at = (j % peer * 3 + g) * side
    return tile_ref[j // peer, at:at + side]


def local_kernel(dims, row_ref, col_ref, row_to_ref, col_to_ref, tok_ref, grad_ref, tile_ref, out_ref,
                 pre, back, hid, pair, acc_out, acc_in):
    rows, cols, owners, side, peer, group = dims
    phase, block = pl.program_id(0), pl.program_id(1)
    blocks = pl.num_programs(1)
    per = rows // owners

    @pl.when((phase == 0) & (block == 0))
    def _():
        @pl.loop(0, cols)
        def _(i):
            pre[i] = jnp.zeros(pre.shape[1:], F32)
            back[i] = jnp.zeros(back.shape[1:], F32)

    @pl.when(phase == 0)
    def _():
        for j in range(group):
            s = block * group + j
            at = pl.ds(pl.multiple_of(row_ref[s] * side, side), side)
            to = col_to_ref[s]
            both = jnp.concatenate([tile_of(tile_ref, peer, j, 0), tile_of(tile_ref, peer, j, 1)], axis=1)
            pre[to] += jnp.dot(tok_ref[:, at], both, preferred_element_type=F32)
            back[to] += lax.dot_general(grad_ref[:, at], tile_of(tile_ref, peer, j, 2), NT, preferred_element_type=F32)

    @pl.when((phase == 1) & (block == 0))
    def _():
        @pl.loop(0, cols)
        def _(i):
            gate = pre[i, :, :side]
            up = pre[i, :, side:]
            gh = back[i]
            s = jax.nn.sigmoid(gate)
            act = gate * s
            hid[i] = (act * up).astype(jnp.bfloat16)
            pair[i, :, :side] = (gh * up * (s * (1.0 + gate * (1.0 - s)))).astype(jnp.bfloat16)
            pair[i, :, side:] = (gh * act).astype(jnp.bfloat16)

        @pl.loop(0, rows)
        def _(i):
            acc_out[i] = jnp.zeros(acc_out.shape[1:], F32)
            acc_in[i] = jnp.zeros(acc_in.shape[1:], F32)

    @pl.when(phase == 1)
    def _():
        for j in range(group):
            s = block * group + j
            c = col_ref[s]
            to = row_to_ref[s]
            both = jnp.concatenate([tile_of(tile_ref, peer, j, 0), tile_of(tile_ref, peer, j, 1)], axis=1)
            acc_out[to] += jnp.dot(hid[c], tile_of(tile_ref, peer, j, 2), preferred_element_type=F32)
            acc_in[to] += lax.dot_general(pair[c], both, NT, preferred_element_type=F32)

    @pl.when((phase == 1) & (block == blocks - 1))
    def _():
        @pl.loop(0, owners)
        def _(k):
            for i in range(per):
                out_ref[k, 0, i] = acc_out[k * per + i].astype(jnp.bfloat16)
                out_ref[k, 1, i] = acc_in[k * per + i].astype(jnp.bfloat16)


def local_pass(tokens, out_grad, tiles, row, col, row_to, col_to, owners, cols, peer):
    toks, feats = tokens.shape
    sources, length, side = tiles.shape
    slots = sources * peer
    rows = feats // side
    whole = lambda p, b, *_: (0, 0)
    once = pl.Buffered(1)
    return pl.pallas_call(
        functools.partial(local_kernel, (rows, cols, owners, side, peer, GROUP)),
        out_shape=jax.ShapeDtypeStruct((owners, 2, rows // owners, toks, side), jnp.bfloat16),
        grid_spec=pltpu.PrefetchScalarGridSpec(
            num_scalar_prefetch=4,
            grid=(2, slots // GROUP),
            in_specs=[
                pl.BlockSpec((toks, feats), whole, pipeline_mode=once),
                pl.BlockSpec((toks, feats), whole, pipeline_mode=once),
                pl.BlockSpec((GROUP // peer, length, side), lambda p, b, *_: (b, 0, 0)),
            ],
            out_specs=pl.BlockSpec((owners, 2, rows // owners, toks, side), lambda p, b, *_: (0, 0, 0, 0, 0), pipeline_mode=once),
            scratch_shapes=[
                pltpu.VMEM((cols + 1, toks, 2 * side), F32),
                pltpu.VMEM((cols + 1, toks, side), F32),
                pltpu.VMEM((cols, toks, side), jnp.bfloat16),
                pltpu.VMEM((cols, toks, 2 * side), jnp.bfloat16),
                pltpu.VMEM((rows + 1, toks, side), F32),
                pltpu.VMEM((rows + 1, toks, side), F32),
            ],
        ),
        compiler_params=pltpu.CompilerParams(vmem_limit_bytes=58 * 2**20),
        cost_estimate=pl.CostEstimate(flops=12 * slots * toks * side * side, bytes_accessed=30 * 2**20, transcendentals=0),
    )(row, col, row_to, col_to, tokens, out_grad, tiles)


def body(tokens, out_grad, weight_tiles, tile_places, live_counts):
    toks, feats = tokens.shape
    side = weight_tiles.shape[-1]
    peer = weight_tiles.shape[1]
    rows = feats // side
    owners = lax.axis_size("tensor")
    cols = FF // (side * owners)
    n_dp = lax.axis_size("dp")
    live = jnp.arange(peer)[None, :] < live_counts[:, None]
    meta = jnp.concatenate([tile_places // cols, tile_places % cols, live.astype(jnp.int32)], axis=1)
    meta = jnp.pad(meta.astype(jnp.bfloat16), ((0, 0), (0, side - 3 * peer)))
    meta = jnp.broadcast_to(meta[:, None, :], (owners, META, side))
    blocks = jnp.concatenate([weight_tiles.reshape(owners, -1, side), meta], axis=1)
    tiles = spread(blocks, n_dp)
    tiles = tiles.reshape((n_dp * owners,) + tiles.shape[2:])
    meta = tiles[:, -META, :3 * peer].astype(jnp.int32)
    row = meta[:, :peer].reshape(-1)
    col = meta[:, peer:2 * peer].reshape(-1)
    live = meta[:, 2 * peer:].reshape(-1) > 0
    row_to = jnp.where(live, row, rows)
    col_to = jnp.where(live, col, cols)
    parts = local_pass(tokens, out_grad, tiles, row, col, row_to, col_to, owners, cols, peer)
    if (n_dp, owners) == (4, 8):
        return line_sum(parts)
    total = lax.psum_scatter(parts, "tensor", scatter_dimension=0, tiled=True)
    total = jnp.transpose(total[0], (0, 2, 1, 3)).reshape(2, toks, feats // owners)
    return total[0], total[1]


def solution(mesh):
    in_specs = (
        P("dp", None),
        P("dp", None),
        P(("dp", "tensor"), None, None, None, None),
        P(("dp", "tensor"), None),
        P(("dp", "tensor")),
    )
    out_specs = (P("dp", "tensor"), P("dp", "tensor"))
    return jax.shard_map(body, mesh=mesh, in_specs=in_specs, out_specs=out_specs, check_vma=False)
```

```python
import functools

import jax
import jax.numpy as jnp
from jax import lax
from jax.experimental import pallas as pl
from jax.experimental.pallas import tpu as pltpu
from jax.sharding import PartitionSpec as P

FF = 26624
GROUP = 8
F32 = jnp.float32
NT = (((1,), (1,)), ((), ()))
MESH = pl.DeviceIdType.MESH
META = 16


def near_first(n):
    order = []
    for o in range(1, n // 2 + 1):
        order += [o] if 2 * o == n else [o, n - o]
    return order


def spread_kernel(n_dp, owners, block_ref, out_ref, own_sem, send_a, recv_a, send_b, recv_b):
    d, t = lax.axis_index("dp"), lax.axis_index("tensor")
    barrier = pltpu.get_barrier_semaphore()
    for o in range(1, owners):
        pl.semaphore_signal(barrier, inc=1, device_id=(d, lax.rem(t + o, owners)), device_id_type=MESH)
    for e in range(1, n_dp):
        pl.semaphore_signal(barrier, inc=1, device_id=(lax.rem(d + e, n_dp), t), device_id_type=MESH)
    pl.semaphore_wait(barrier, owners - 1 + n_dp - 1)

    own = pltpu.make_async_copy(block_ref.at[t], out_ref.at[d, t], own_sem)
    own.start()
    first, second = {}, []

    def forward(src, slot, o):
        for e in range(1, n_dp):
            copy = pltpu.make_async_remote_copy(
                src_ref=src, dst_ref=out_ref.at[d, slot],
                send_sem=send_b.at[e - 1, o], recv_sem=recv_b.at[e - 1, o],
                device_id=(lax.rem(d + e, n_dp), t), device_id_type=MESH)
            copy.start()
            second.append(copy)

    order = near_first(owners)
    for o in order:
        to = lax.rem(t + o, owners)
        first[o] = pltpu.make_async_remote_copy(
            src_ref=block_ref.at[to], dst_ref=out_ref.at[d, t],
            send_sem=send_a.at[o - 1], recv_sem=recv_a.at[o - 1],
            device_id=(d, to), device_id_type=MESH)
        first[o].start()
    forward(block_ref.at[t], t, 0)
    for o in order:
        first[o].wait_recv()
        slot = lax.rem(t + owners - o, owners)
        forward(out_ref.at[d, slot], slot, o)
    own.wait()
    for o in order:
        first[o].wait_send()
    for copy in second:
        copy.wait()


def square_kernel(n_dp, owners, block_ref, out_ref, own_sem, send_a, recv_a, send_b, recv_b):
    d, t = lax.axis_index("dp"), lax.axis_index("tensor")
    beside = (d + 1 - 2 * lax.rem(d, 2), lax.rem(d + 2, 4))
    barrier = pltpu.get_barrier_semaphore()
    for o in range(1, owners):
        pl.semaphore_signal(barrier, inc=1, device_id=(d, lax.rem(t + o, owners)), device_id_type=MESH)
    for to in beside:
        pl.semaphore_signal(barrier, inc=1, device_id=(to, t), device_id_type=MESH)
    pl.semaphore_wait(barrier, owners - 1 + 2)

    def send(src, row, slot, to, kind, o):
        copy = pltpu.make_async_remote_copy(
            src_ref=src, dst_ref=out_ref.at[row, slot],
            send_sem=send_b.at[kind, o], recv_sem=recv_b.at[kind, o],
            device_id=(to, t), device_id_type=MESH)
        copy.start()
        return copy

    order = near_first(owners)
    first, direct, passed = {}, {}, []

    def outward(src, o):
        slot = lax.rem(t + owners - o, owners)
        direct[o] = [send(src, d, slot, beside[kind], kind, o) for kind in range(2)]

    def onward(i, o):
        slot = lax.rem(t + owners - o, owners)
        via = i % 2
        direct[o][via].wait_recv()
        passed.append(send(out_ref.at[beside[via], slot], beside[via], slot, beside[1 - via], 2, o))

    outward(block_ref.at[t], 0)
    for o in order:
        to = lax.rem(t + o, owners)
        first[o] = pltpu.make_async_remote_copy(
            src_ref=block_ref.at[to], dst_ref=out_ref.at[d, t],
            send_sem=send_a.at[o - 1], recv_sem=recv_a.at[o - 1],
            device_id=(d, to), device_id_type=MESH)
        first[o].start()
    own = pltpu.make_async_copy(block_ref.at[t], out_ref.at[d, t], own_sem)
    own.start()
    turns = [0] + order
    lag = 2
    for i in range(len(turns) + lag):
        if 0 < i < len(turns):
            o = turns[i]
            first[o].wait_recv()
            outward(out_ref.at[d, lax.rem(t + owners - o, owners)], o)
        if i >= lag:
            onward(i - lag, turns[i - lag])
    own.wait()
    for o in order:
        first[o].wait_send()
    for i, o in enumerate(turns):
        direct[o][1 - i % 2].wait_recv()
        direct[o][0].wait_send()
        direct[o][1].wait_send()
    for copy in passed:
        copy.wait()


def spread(blocks, n_dp):
    owners, length, side = blocks.shape
    return pl.pallas_call(
        functools.partial(square_kernel if n_dp == 4 else spread_kernel, n_dp, owners),
        out_shape=jax.ShapeDtypeStruct((n_dp, owners, length, side), blocks.dtype),
        in_specs=[pl.BlockSpec(memory_space=pl.ANY)],
        out_specs=pl.BlockSpec(memory_space=pl.ANY),
        scratch_shapes=[
            pltpu.SemaphoreType.DMA(()),
            pltpu.SemaphoreType.DMA((owners - 1,)),
            pltpu.SemaphoreType.DMA((owners - 1,)),
            pltpu.SemaphoreType.DMA((n_dp - 1, owners)),
            pltpu.SemaphoreType.DMA((n_dp - 1, owners)),
        ],
        compiler_params=pltpu.CompilerParams(collective_id=0, has_side_effects=True),
        cost_estimate=pl.CostEstimate(flops=0, bytes_accessed=2 * n_dp * blocks.size * 2, transcendentals=0),
    )(blocks)


def line_kernel(chips, chunks, part_ref, out_ref, in_ref, own_buf, mate_buf, sent, from_buf,
                own_sem, mate_send, mate_recv, line_send, line_recv):
    d, t = lax.axis_index("dp"), lax.axis_index("tensor")
    z, c = t // 2, lax.rem(t, 2)
    owners, last = 2 * chips, chips - 1
    mate = t + 1 - 2 * c
    tiles = part_ref.shape[1]
    size = tiles // chunks
    half = tiles // 2
    side = part_ref.shape[-1]
    onward = (lax.rem(t + 2, owners), lax.rem(t + owners - 2, owners))
    has_next = (z < last, z > 0)
    has_before = (z > 0, z < last)

    barrier = pltpu.get_barrier_semaphore()
    pl.semaphore_signal(barrier, inc=1, device_id=(d, mate), device_id_type=MESH)
    for way in range(2):
        @pl.when(has_next[way])
        def _():
            pl.semaphore_signal(barrier, inc=1, device_id=(d, onward[way]), device_id_type=MESH)
    inner = (z > 0) & (z < last)

    @pl.when(inner)
    def _():
        pl.semaphore_wait(barrier, 3)

    @pl.when(jnp.logical_not(inner))
    def _():
        pl.semaphore_wait(barrier, 2)

    swaps, loads = {}, {}
    order = []
    for k in range(chips // 2):
        order += [last - k, k]
    for to in order:
        swaps[to] = pltpu.make_async_remote_copy(
            src_ref=part_ref.at[2 * to + 1 - c], dst_ref=mate_buf.at[to],
            send_sem=mate_send.at[to], recv_sem=mate_recv.at[to],
            device_id=(d, mate), device_id_type=MESH)
        swaps[to].start()
        loads[to] = pltpu.make_async_copy(part_ref.at[2 * to + c], own_buf.at[to], own_sem.at[to])
        loads[to].start()

    def hop(way, to, q):
        at = pl.ds(q * size, size)
        return pltpu.make_async_remote_copy(
            src_ref=sent.at[to, at], dst_ref=from_buf.at[way, to, at],
            send_sem=line_send.at[way, to, q], recv_sem=line_recv.at[way, to, q],
            device_id=(d, onward[way]), device_id_type=MESH)

    def own_sum(to, i):
        return own_buf[to, i].astype(F32) + mate_buf[to, i].astype(F32)

    for k in range(last):
        for to in order[2 * k:2 * k + 2]:
            loads[to].wait()
            swaps[to].wait_recv()

        @pl.loop(0, chunks)
        def _(q):
            for way, to in ((0, last - k), (1, k)):
                goes = (z < to) if way == 0 else (z > to)

                @pl.when(goes & has_before[way])
                def _():
                    hop(way, to, q).wait_recv()
                    for j in range(size):
                        i = q * size + j
                        sent[to, i] = (own_sum(to, i) + from_buf[way, to, i].astype(F32)).astype(jnp.bfloat16)
                    hop(way, to, q).start()

                @pl.when(goes & jnp.logical_not(has_before[way]))
                def _():
                    for j in range(size):
                        i = q * size + j
                        sent[to, i] = own_sum(to, i).astype(jnp.bfloat16)
                    hop(way, to, q).start()

    def finish(ways):
        for q in range(chunks):
            for way in ways:
                hop(way, z, q).wait_recv()
            for j in range(size):
                i = q * size + j
                total = own_sum(z, i)
                for way in ways:
                    total = total + from_buf[way, z, i].astype(F32)
                to_ref = out_ref if i < half else in_ref
                col = i % half * side
                to_ref[:, col:col + side] = total.astype(jnp.bfloat16)

    @pl.when(z == 0)
    def _():
        finish((1,))

    @pl.when(z == last)
    def _():
        finish((0,))

    @pl.when((z > 0) & (z < last))
    def _():
        finish((0, 1))

    for to in order:
        swaps[to].wait_send()
    for k in range(last):
        @pl.loop(0, chunks)
        def _(q):
            for way, to in ((0, last - k), (1, k)):
                goes = (z < to) if way == 0 else (z > to)

                @pl.when(goes)
                def _():
                    hop(way, to, q).wait_send()


def line_sum(parts, chunks=8):
    owners, _, per, toks, side = parts.shape
    chips, tiles = owners // 2, 2 * per
    parts = parts.reshape(owners, tiles, toks, side)
    result = jax.ShapeDtypeStruct((toks, per * side), jnp.bfloat16)
    vmem = pl.BlockSpec(memory_space=pltpu.VMEM)
    return pl.pallas_call(
        functools.partial(line_kernel, chips, chunks),
        out_shape=(result, result),
        in_specs=[pl.BlockSpec(memory_space=pl.ANY)],
        out_specs=(vmem, vmem),
        scratch_shapes=[
            pltpu.VMEM((chips, tiles, toks, side), jnp.bfloat16),
            pltpu.VMEM((chips, tiles, toks, side), jnp.bfloat16),
            pltpu.VMEM((chips, tiles, toks, side), jnp.bfloat16),
            pltpu.VMEM((2, chips, tiles, toks, side), jnp.bfloat16),
            pltpu.SemaphoreType.DMA((chips,)),
            pltpu.SemaphoreType.DMA((chips,)),
            pltpu.SemaphoreType.DMA((chips,)),
            pltpu.SemaphoreType.DMA((2, chips, chunks)),
            pltpu.SemaphoreType.DMA((2, chips, chunks)),
        ],
        compiler_params=pltpu.CompilerParams(collective_id=1, has_side_effects=True, vmem_limit_bytes=58 * 2**20),
        cost_estimate=pl.CostEstimate(flops=parts.size, bytes_accessed=2 * parts.size, transcendentals=0),
    )(parts)


def tile_of(tile_ref, peer, j, g):
    side = tile_ref.shape[-1]
    at = (j % peer * 3 + g) * side
    return tile_ref[j // peer, at:at + side]


def local_kernel(dims, row_ref, col_ref, row_to_ref, col_to_ref, tok_ref, grad_ref, tile_ref, out_ref,
                 pre, back, hid, pair, acc_out, acc_in):
    rows, cols, owners, side, peer, group = dims
    phase, block = pl.program_id(0), pl.program_id(1)
    blocks = pl.num_programs(1)
    per = rows // owners

    @pl.when((phase == 0) & (block == 0))
    def _():
        @pl.loop(0, cols)
        def _(i):
            pre[i] = jnp.zeros(pre.shape[1:], F32)
            back[i] = jnp.zeros(back.shape[1:], F32)

    @pl.when(phase == 0)
    def _():
        for j in range(group):
            s = block * group + j
            at = pl.ds(pl.multiple_of(row_ref[s] * side, side), side)
            to = col_to_ref[s]
            both = jnp.concatenate([tile_of(tile_ref, peer, j, 0), tile_of(tile_ref, peer, j, 1)], axis=1)
            pre[to] += jnp.dot(tok_ref[:, at], both, preferred_element_type=F32)
            back[to] += lax.dot_general(grad_ref[:, at], tile_of(tile_ref, peer, j, 2), NT, preferred_element_type=F32)

    @pl.when((phase == 1) & (block == 0))
    def _():
        @pl.loop(0, cols)
        def _(i):
            gate = pre[i, :, :side]
            up = pre[i, :, side:]
            gh = back[i]
            s = jax.nn.sigmoid(gate)
            act = gate * s
            hid[i] = (act * up).astype(jnp.bfloat16)
            pair[i, :, :side] = (gh * up * (s * (1.0 + gate * (1.0 - s)))).astype(jnp.bfloat16)
            pair[i, :, side:] = (gh * act).astype(jnp.bfloat16)

        @pl.loop(0, rows)
        def _(i):
            acc_out[i] = jnp.zeros(acc_out.shape[1:], F32)
            acc_in[i] = jnp.zeros(acc_in.shape[1:], F32)

    @pl.when(phase == 1)
    def _():
        for j in range(group):
            s = block * group + j
            c = col_ref[s]
            to = row_to_ref[s]
            both = jnp.concatenate([tile_of(tile_ref, peer, j, 0), tile_of(tile_ref, peer, j, 1)], axis=1)
            acc_out[to] += jnp.dot(hid[c], tile_of(tile_ref, peer, j, 2), preferred_element_type=F32)
            acc_in[to] += lax.dot_general(pair[c], both, NT, preferred_element_type=F32)

    @pl.when((phase == 1) & (block == blocks - 1))
    def _():
        @pl.loop(0, owners)
        def _(k):
            for i in range(per):
                out_ref[k, 0, i] = acc_out[k * per + i].astype(jnp.bfloat16)
                out_ref[k, 1, i] = acc_in[k * per + i].astype(jnp.bfloat16)


def local_pass(tokens, out_grad, tiles, row, col, row_to, col_to, owners, cols, peer):
    toks, feats = tokens.shape
    sources, length, side = tiles.shape
    slots = sources * peer
    rows = feats // side
    whole = lambda p, b, *_: (0, 0)
    once = pl.Buffered(1)
    return pl.pallas_call(
        functools.partial(local_kernel, (rows, cols, owners, side, peer, GROUP)),
        out_shape=jax.ShapeDtypeStruct((owners, 2, rows // owners, toks, side), jnp.bfloat16),
        grid_spec=pltpu.PrefetchScalarGridSpec(
            num_scalar_prefetch=4,
            grid=(2, slots // GROUP),
            in_specs=[
                pl.BlockSpec((toks, feats), whole, pipeline_mode=once),
                pl.BlockSpec((toks, feats), whole, pipeline_mode=once),
                pl.BlockSpec((GROUP // peer, length, side), lambda p, b, *_: (b, 0, 0)),
            ],
            out_specs=pl.BlockSpec((owners, 2, rows // owners, toks, side), lambda p, b, *_: (0, 0, 0, 0, 0), pipeline_mode=once),
            scratch_shapes=[
                pltpu.VMEM((cols + 1, toks, 2 * side), F32),
                pltpu.VMEM((cols + 1, toks, side), F32),
                pltpu.VMEM((cols, toks, side), jnp.bfloat16),
                pltpu.VMEM((cols, toks, 2 * side), jnp.bfloat16),
                pltpu.VMEM((rows + 1, toks, side), F32),
                pltpu.VMEM((rows + 1, toks, side), F32),
            ],
        ),
        compiler_params=pltpu.CompilerParams(vmem_limit_bytes=58 * 2**20),
        cost_estimate=pl.CostEstimate(flops=12 * slots * toks * side * side, bytes_accessed=30 * 2**20, transcendentals=0),
    )(row, col, row_to, col_to, tokens, out_grad, tiles)


def body(tokens, out_grad, weight_tiles, tile_places, live_counts):
    toks, feats = tokens.shape
    side = weight_tiles.shape[-1]
    peer = weight_tiles.shape[1]
    rows = feats // side
    owners = lax.axis_size("tensor")
    cols = FF // (side * owners)
    n_dp = lax.axis_size("dp")
    live = jnp.arange(peer)[None, :] < live_counts[:, None]
    meta = jnp.concatenate([tile_places // cols, tile_places % cols, live.astype(jnp.int32)], axis=1)
    meta = jnp.pad(meta.astype(jnp.bfloat16), ((0, 0), (0, side - 3 * peer)))
    meta = jnp.broadcast_to(meta[:, None, :], (owners, META, side))
    blocks = jnp.concatenate([weight_tiles.reshape(owners, -1, side), meta], axis=1)
    tiles = spread(blocks, n_dp)
    tiles = tiles.reshape((n_dp * owners,) + tiles.shape[2:])
    meta = tiles[:, -META, :3 * peer].astype(jnp.int32)
    row = meta[:, :peer].reshape(-1)
    col = meta[:, peer:2 * peer].reshape(-1)
    live = meta[:, 2 * peer:].reshape(-1) > 0
    row_to = jnp.where(live, row, rows)
    col_to = jnp.where(live, col, cols)
    parts = local_pass(tokens, out_grad, tiles, row, col, row_to, col_to, owners, cols, peer)
    if (n_dp, owners) == (4, 8):
        return line_sum(parts)
    total = lax.psum_scatter(parts, "tensor", scatter_dimension=0, tiled=True)
    total = jnp.transpose(total[0], (0, 2, 1, 3)).reshape(2, toks, feats // owners)
    return total[0], total[1]


def solution(mesh):
    in_specs = (
        P("dp", None),
        P("dp", None),
        P(("dp", "tensor"), None, None, None, None),
        P(("dp", "tensor"), None),
        P(("dp", "tensor")),
    )
    out_specs = (P("dp", "tensor"), P("dp", "tensor"))
    return jax.shard_map(body, mesh=mesh, in_specs=in_specs, out_specs=out_specs, check_vma=False)
```

```python
import functools

import jax
import jax.numpy as jnp
from jax import lax
from jax.experimental import pallas as pl
from jax.experimental.pallas import tpu as pltpu
from jax.sharding import PartitionSpec as P

FF = 26624
GROUP = 16
F32 = jnp.float32
NT = (((1,), (1,)), ((), ()))
MESH = pl.DeviceIdType.MESH
META = 16


def near_first(n):
    order = []
    for o in range(1, n // 2 + 1):
        order += [o] if 2 * o == n else [o, n - o]
    return order


def spread_kernel(n_dp, owners, block_ref, out_ref, own_sem, send_a, recv_a, send_b, recv_b):
    d, t = lax.axis_index("dp"), lax.axis_index("tensor")
    barrier = pltpu.get_barrier_semaphore()
    for o in range(1, owners):
        pl.semaphore_signal(barrier, inc=1, device_id=(d, lax.rem(t + o, owners)), device_id_type=MESH)
    for e in range(1, n_dp):
        pl.semaphore_signal(barrier, inc=1, device_id=(lax.rem(d + e, n_dp), t), device_id_type=MESH)
    pl.semaphore_wait(barrier, owners - 1 + n_dp - 1)

    own = pltpu.make_async_copy(block_ref.at[t], out_ref.at[d, t], own_sem)
    own.start()
    first, second = {}, []

    def forward(src, slot, o):
        for e in range(1, n_dp):
            copy = pltpu.make_async_remote_copy(
                src_ref=src, dst_ref=out_ref.at[d, slot],
                send_sem=send_b.at[e - 1, o], recv_sem=recv_b.at[e - 1, o],
                device_id=(lax.rem(d + e, n_dp), t), device_id_type=MESH)
            copy.start()
            second.append(copy)

    order = near_first(owners)
    for o in order:
        to = lax.rem(t + o, owners)
        first[o] = pltpu.make_async_remote_copy(
            src_ref=block_ref.at[to], dst_ref=out_ref.at[d, t],
            send_sem=send_a.at[o - 1], recv_sem=recv_a.at[o - 1],
            device_id=(d, to), device_id_type=MESH)
        first[o].start()
    forward(block_ref.at[t], t, 0)
    for o in order:
        first[o].wait_recv()
        slot = lax.rem(t + owners - o, owners)
        forward(out_ref.at[d, slot], slot, o)
    own.wait()
    for o in order:
        first[o].wait_send()
    for copy in second:
        copy.wait()


def square_kernel(n_dp, owners, block_ref, out_ref, own_sem, send_a, recv_a, send_b, recv_b):
    d, t = lax.axis_index("dp"), lax.axis_index("tensor")
    beside = (d + 1 - 2 * lax.rem(d, 2), lax.rem(d + 2, 4))
    barrier = pltpu.get_barrier_semaphore()
    for o in range(1, owners):
        pl.semaphore_signal(barrier, inc=1, device_id=(d, lax.rem(t + o, owners)), device_id_type=MESH)
    for to in beside:
        pl.semaphore_signal(barrier, inc=1, device_id=(to, t), device_id_type=MESH)
    pl.semaphore_wait(barrier, owners - 1 + 2)

    def send(src, row, slot, to, kind, o):
        copy = pltpu.make_async_remote_copy(
            src_ref=src, dst_ref=out_ref.at[row, slot],
            send_sem=send_b.at[kind, o], recv_sem=recv_b.at[kind, o],
            device_id=(to, t), device_id_type=MESH)
        copy.start()
        return copy

    order = near_first(owners)
    first, direct, passed = {}, {}, []

    def outward(src, o):
        slot = lax.rem(t + owners - o, owners)
        direct[o] = [send(src, d, slot, beside[kind], kind, o) for kind in range(2)]

    def onward(i, o):
        slot = lax.rem(t + owners - o, owners)
        via = i % 2
        direct[o][via].wait_recv()
        passed.append(send(out_ref.at[beside[via], slot], beside[via], slot, beside[1 - via], 2, o))

    outward(block_ref.at[t], 0)
    for o in order:
        to = lax.rem(t + o, owners)
        first[o] = pltpu.make_async_remote_copy(
            src_ref=block_ref.at[to], dst_ref=out_ref.at[d, t],
            send_sem=send_a.at[o - 1], recv_sem=recv_a.at[o - 1],
            device_id=(d, to), device_id_type=MESH)
        first[o].start()
    own = pltpu.make_async_copy(block_ref.at[t], out_ref.at[d, t], own_sem)
    own.start()
    turns = [0] + order
    lag = 2
    for i in range(len(turns) + lag):
        if 0 < i < len(turns):
            o = turns[i]
            first[o].wait_recv()
            outward(out_ref.at[d, lax.rem(t + owners - o, owners)], o)
        if i >= lag:
            onward(i - lag, turns[i - lag])
    own.wait()
    for o in order:
        first[o].wait_send()
    for i, o in enumerate(turns):
        direct[o][1 - i % 2].wait_recv()
        direct[o][0].wait_send()
        direct[o][1].wait_send()
    for copy in passed:
        copy.wait()


def spread(blocks, n_dp):
    owners, length, side = blocks.shape
    return pl.pallas_call(
        functools.partial(square_kernel if n_dp == 4 else spread_kernel, n_dp, owners),
        out_shape=jax.ShapeDtypeStruct((n_dp, owners, length, side), blocks.dtype),
        in_specs=[pl.BlockSpec(memory_space=pl.ANY)],
        out_specs=pl.BlockSpec(memory_space=pl.ANY),
        scratch_shapes=[
            pltpu.SemaphoreType.DMA(()),
            pltpu.SemaphoreType.DMA((owners - 1,)),
            pltpu.SemaphoreType.DMA((owners - 1,)),
            pltpu.SemaphoreType.DMA((n_dp - 1, owners)),
            pltpu.SemaphoreType.DMA((n_dp - 1, owners)),
        ],
        compiler_params=pltpu.CompilerParams(collective_id=0, has_side_effects=True),
        cost_estimate=pl.CostEstimate(flops=0, bytes_accessed=2 * n_dp * blocks.size * 2, transcendentals=0),
    )(blocks)


def line_kernel(chips, chunks, part_ref, out_ref, in_ref, own_buf, mate_buf, sent, from_buf,
                own_sem, mate_send, mate_recv, line_send, line_recv):
    d, t = lax.axis_index("dp"), lax.axis_index("tensor")
    z, c = t // 2, lax.rem(t, 2)
    owners, last = 2 * chips, chips - 1
    mate = t + 1 - 2 * c
    tiles = part_ref.shape[1]
    size = tiles // chunks
    half = tiles // 2
    side = part_ref.shape[-1]
    onward = (lax.rem(t + 2, owners), lax.rem(t + owners - 2, owners))
    has_next = (z < last, z > 0)
    has_before = (z > 0, z < last)

    barrier = pltpu.get_barrier_semaphore()
    pl.semaphore_signal(barrier, inc=1, device_id=(d, mate), device_id_type=MESH)
    for way in range(2):
        @pl.when(has_next[way])
        def _():
            pl.semaphore_signal(barrier, inc=1, device_id=(d, onward[way]), device_id_type=MESH)
    inner = (z > 0) & (z < last)

    @pl.when(inner)
    def _():
        pl.semaphore_wait(barrier, 3)

    @pl.when(jnp.logical_not(inner))
    def _():
        pl.semaphore_wait(barrier, 2)

    swaps, loads = {}, {}
    order = []
    for k in range(chips // 2):
        order += [last - k, k]
    for to in order:
        swaps[to] = pltpu.make_async_remote_copy(
            src_ref=part_ref.at[2 * to + 1 - c], dst_ref=mate_buf.at[to],
            send_sem=mate_send.at[to], recv_sem=mate_recv.at[to],
            device_id=(d, mate), device_id_type=MESH)
        swaps[to].start()
        loads[to] = pltpu.make_async_copy(part_ref.at[2 * to + c], own_buf.at[to], own_sem.at[to])
        loads[to].start()

    def hop(way, to, q):
        at = pl.ds(q * size, size)
        return pltpu.make_async_remote_copy(
            src_ref=sent.at[to, at], dst_ref=from_buf.at[way, to, at],
            send_sem=line_send.at[way, to, q], recv_sem=line_recv.at[way, to, q],
            device_id=(d, onward[way]), device_id_type=MESH)

    def own_sum(to, i):
        return own_buf[to, i].astype(F32) + mate_buf[to, i].astype(F32)

    for k in range(last):
        for to in order[2 * k:2 * k + 2]:
            loads[to].wait()
            swaps[to].wait_recv()

        @pl.loop(0, chunks)
        def _(q):
            for way, to in ((0, last - k), (1, k)):
                goes = (z < to) if way == 0 else (z > to)

                @pl.when(goes & has_before[way])
                def _():
                    hop(way, to, q).wait_recv()
                    for j in range(size):
                        i = q * size + j
                        sent[to, i] = (own_sum(to, i) + from_buf[way, to, i].astype(F32)).astype(jnp.bfloat16)
                    hop(way, to, q).start()

                @pl.when(goes & jnp.logical_not(has_before[way]))
                def _():
                    for j in range(size):
                        i = q * size + j
                        sent[to, i] = own_sum(to, i).astype(jnp.bfloat16)
                    hop(way, to, q).start()

    def finish(ways):
        for q in range(chunks):
            for way in ways:
                hop(way, z, q).wait_recv()
            for j in range(size):
                i = q * size + j
                total = own_sum(z, i)
                for way in ways:
                    total = total + from_buf[way, z, i].astype(F32)
                to_ref = out_ref if i < half else in_ref
                col = i % half * side
                to_ref[:, col:col + side] = total.astype(jnp.bfloat16)

    @pl.when(z == 0)
    def _():
        finish((1,))

    @pl.when(z == last)
    def _():
        finish((0,))

    @pl.when((z > 0) & (z < last))
    def _():
        finish((0, 1))

    for to in order:
        swaps[to].wait_send()
    for k in range(last):
        @pl.loop(0, chunks)
        def _(q):
            for way, to in ((0, last - k), (1, k)):
                goes = (z < to) if way == 0 else (z > to)

                @pl.when(goes)
                def _():
                    hop(way, to, q).wait_send()


def line_sum(parts, chunks=4):
    owners, _, per, toks, side = parts.shape
    chips, tiles = owners // 2, 2 * per
    parts = parts.reshape(owners, tiles, toks, side)
    result = jax.ShapeDtypeStruct((toks, per * side), jnp.bfloat16)
    vmem = pl.BlockSpec(memory_space=pltpu.VMEM)
    return pl.pallas_call(
        functools.partial(line_kernel, chips, chunks),
        out_shape=(result, result),
        in_specs=[pl.BlockSpec(memory_space=pl.ANY)],
        out_specs=(vmem, vmem),
        scratch_shapes=[
            pltpu.VMEM((chips, tiles, toks, side), jnp.bfloat16),
            pltpu.VMEM((chips, tiles, toks, side), jnp.bfloat16),
            pltpu.VMEM((chips, tiles, toks, side), jnp.bfloat16),
            pltpu.VMEM((2, chips, tiles, toks, side), jnp.bfloat16),
            pltpu.SemaphoreType.DMA((chips,)),
            pltpu.SemaphoreType.DMA((chips,)),
            pltpu.SemaphoreType.DMA((chips,)),
            pltpu.SemaphoreType.DMA((2, chips, chunks)),
            pltpu.SemaphoreType.DMA((2, chips, chunks)),
        ],
        compiler_params=pltpu.CompilerParams(collective_id=1, has_side_effects=True, vmem_limit_bytes=58 * 2**20),
        cost_estimate=pl.CostEstimate(flops=parts.size, bytes_accessed=2 * parts.size, transcendentals=0),
    )(parts)


def tile_of(tile_ref, peer, j, g):
    side = tile_ref.shape[-1]
    at = (j % peer * 3 + g) * side
    return tile_ref[j // peer, at:at + side]


def local_kernel(dims, row_ref, col_ref, row_to_ref, col_to_ref, tok_ref, grad_ref, tile_ref, out_ref,
                 pre, back, hid, pair, acc_out, acc_in):
    rows, cols, owners, side, peer, group = dims
    phase, block = pl.program_id(0), pl.program_id(1)
    blocks = pl.num_programs(1)
    per = rows // owners

    @pl.when((phase == 0) & (block == 0))
    def _():
        @pl.loop(0, cols)
        def _(i):
            pre[i] = jnp.zeros(pre.shape[1:], F32)
            back[i] = jnp.zeros(back.shape[1:], F32)

    @pl.when(phase == 0)
    def _():
        for j in range(group):
            s = block * group + j
            at = pl.ds(pl.multiple_of(row_ref[s] * side, side), side)
            to = col_to_ref[s]
            both = jnp.concatenate([tile_of(tile_ref, peer, j, 0), tile_of(tile_ref, peer, j, 1)], axis=1)
            pre[to] += jnp.dot(tok_ref[:, at], both, preferred_element_type=F32)
            back[to] += lax.dot_general(grad_ref[:, at], tile_of(tile_ref, peer, j, 2), NT, preferred_element_type=F32)

    @pl.when((phase == 1) & (block == 0))
    def _():
        @pl.loop(0, cols)
        def _(i):
            gate = pre[i, :, :side]
            up = pre[i, :, side:]
            gh = back[i]
            s = jax.nn.sigmoid(gate)
            act = gate * s
            hid[i] = (act * up).astype(jnp.bfloat16)
            pair[i, :, :side] = (gh * up * (s * (1.0 + gate * (1.0 - s)))).astype(jnp.bfloat16)
            pair[i, :, side:] = (gh * act).astype(jnp.bfloat16)

        @pl.loop(0, rows)
        def _(i):
            acc_out[i] = jnp.zeros(acc_out.shape[1:], F32)
            acc_in[i] = jnp.zeros(acc_in.shape[1:], F32)

    @pl.when(phase == 1)
    def _():
        for j in range(group):
            s = block * group + j
            c = col_ref[s]
            to = row_to_ref[s]
            both = jnp.concatenate([tile_of(tile_ref, peer, j, 0), tile_of(tile_ref, peer, j, 1)], axis=1)
            acc_out[to] += jnp.dot(hid[c], tile_of(tile_ref, peer, j, 2), preferred_element_type=F32)
            acc_in[to] += lax.dot_general(pair[c], both, NT, preferred_element_type=F32)

    @pl.when((phase == 1) & (block == blocks - 1))
    def _():
        @pl.loop(0, owners)
        def _(k):
            for i in range(per):
                out_ref[k, 0, i] = acc_out[k * per + i].astype(jnp.bfloat16)
                out_ref[k, 1, i] = acc_in[k * per + i].astype(jnp.bfloat16)


def local_pass(tokens, out_grad, tiles, row, col, row_to, col_to, owners, cols, peer):
    toks, feats = tokens.shape
    sources, length, side = tiles.shape
    slots = sources * peer
    rows = feats // side
    whole = lambda p, b, *_: (0, 0)
    once = pl.Buffered(1)
    return pl.pallas_call(
        functools.partial(local_kernel, (rows, cols, owners, side, peer, GROUP)),
        out_shape=jax.ShapeDtypeStruct((owners, 2, rows // owners, toks, side), jnp.bfloat16),
        grid_spec=pltpu.PrefetchScalarGridSpec(
            num_scalar_prefetch=4,
            grid=(2, slots // GROUP),
            in_specs=[
                pl.BlockSpec((toks, feats), whole, pipeline_mode=once),
                pl.BlockSpec((toks, feats), whole, pipeline_mode=once),
                pl.BlockSpec((GROUP // peer, length, side), lambda p, b, *_: (b, 0, 0)),
            ],
            out_specs=pl.BlockSpec((owners, 2, rows // owners, toks, side), lambda p, b, *_: (0, 0, 0, 0, 0), pipeline_mode=once),
            scratch_shapes=[
                pltpu.VMEM((cols + 1, toks, 2 * side), F32),
                pltpu.VMEM((cols + 1, toks, side), F32),
                pltpu.VMEM((cols, toks, side), jnp.bfloat16),
                pltpu.VMEM((cols, toks, 2 * side), jnp.bfloat16),
                pltpu.VMEM((rows + 1, toks, side), F32),
                pltpu.VMEM((rows + 1, toks, side), F32),
            ],
        ),
        compiler_params=pltpu.CompilerParams(vmem_limit_bytes=58 * 2**20),
        cost_estimate=pl.CostEstimate(flops=12 * slots * toks * side * side, bytes_accessed=30 * 2**20, transcendentals=0),
    )(row, col, row_to, col_to, tokens, out_grad, tiles)


def body(tokens, out_grad, weight_tiles, tile_places, live_counts):
    toks, feats = tokens.shape
    side = weight_tiles.shape[-1]
    peer = weight_tiles.shape[1]
    rows = feats // side
    owners = lax.axis_size("tensor")
    cols = FF // (side * owners)
    n_dp = lax.axis_size("dp")
    live = jnp.arange(peer)[None, :] < live_counts[:, None]
    meta = jnp.concatenate([tile_places // cols, tile_places % cols, live.astype(jnp.int32)], axis=1)
    meta = jnp.pad(meta.astype(jnp.bfloat16), ((0, 0), (0, side - 3 * peer)))
    meta = jnp.broadcast_to(meta[:, None, :], (owners, META, side))
    blocks = jnp.concatenate([weight_tiles.reshape(owners, -1, side), meta], axis=1)
    tiles = spread(blocks, n_dp)
    tiles = tiles.reshape((n_dp * owners,) + tiles.shape[2:])
    meta = tiles[:, -META, :3 * peer].astype(jnp.int32)
    row = meta[:, :peer].reshape(-1)
    col = meta[:, peer:2 * peer].reshape(-1)
    live = meta[:, 2 * peer:].reshape(-1) > 0
    row_to = jnp.where(live, row, rows)
    col_to = jnp.where(live, col, cols)
    parts = local_pass(tokens, out_grad, tiles, row, col, row_to, col_to, owners, cols, peer)
    if (n_dp, owners) == (4, 8):
        return line_sum(parts)
    total = lax.psum_scatter(parts, "tensor", scatter_dimension=0, tiled=True)
    total = jnp.transpose(total[0], (0, 2, 1, 3)).reshape(2, toks, feats // owners)
    return total[0], total[1]


def solution(mesh):
    in_specs = (
        P("dp", None),
        P("dp", None),
        P(("dp", "tensor"), None, None, None, None),
        P(("dp", "tensor"), None),
        P(("dp", "tensor")),
    )
    out_specs = (P("dp", "tensor"), P("dp", "tensor"))
    return jax.shard_map(body, mesh=mesh, in_specs=in_specs, out_specs=out_specs, check_vma=False)
```

```python
import functools

import jax
import jax.numpy as jnp
from jax import lax
from jax.experimental import pallas as pl
from jax.experimental.pallas import tpu as pltpu
from jax.sharding import PartitionSpec as P

FF = 26624
GROUP = 16
F32 = jnp.float32
NT = (((1,), (1,)), ((), ()))
MESH = pl.DeviceIdType.MESH
META = 16


def near_first(n):
    order = []
    for o in range(1, n // 2 + 1):
        order += [o] if 2 * o == n else [o, n - o]
    return order


def spread_kernel(n_dp, owners, block_ref, out_ref, own_sem, send_a, recv_a, send_b, recv_b):
    d, t = lax.axis_index("dp"), lax.axis_index("tensor")
    barrier = pltpu.get_barrier_semaphore()
    for o in range(1, owners):
        pl.semaphore_signal(barrier, inc=1, device_id=(d, lax.rem(t + o, owners)), device_id_type=MESH)
    for e in range(1, n_dp):
        pl.semaphore_signal(barrier, inc=1, device_id=(lax.rem(d + e, n_dp), t), device_id_type=MESH)
    pl.semaphore_wait(barrier, owners - 1 + n_dp - 1)

    own = pltpu.make_async_copy(block_ref.at[t], out_ref.at[d, t], own_sem)
    own.start()
    first, second = {}, []

    def forward(src, slot, o):
        for e in range(1, n_dp):
            copy = pltpu.make_async_remote_copy(
                src_ref=src, dst_ref=out_ref.at[d, slot],
                send_sem=send_b.at[e - 1, o], recv_sem=recv_b.at[e - 1, o],
                device_id=(lax.rem(d + e, n_dp), t), device_id_type=MESH)
            copy.start()
            second.append(copy)

    order = near_first(owners)
    for o in order:
        to = lax.rem(t + o, owners)
        first[o] = pltpu.make_async_remote_copy(
            src_ref=block_ref.at[to], dst_ref=out_ref.at[d, t],
            send_sem=send_a.at[o - 1], recv_sem=recv_a.at[o - 1],
            device_id=(d, to), device_id_type=MESH)
        first[o].start()
    forward(block_ref.at[t], t, 0)
    for o in order:
        first[o].wait_recv()
        slot = lax.rem(t + owners - o, owners)
        forward(out_ref.at[d, slot], slot, o)
    own.wait()
    for o in order:
        first[o].wait_send()
    for copy in second:
        copy.wait()


def square_kernel(n_dp, owners, block_ref, out_ref, own_sem, send_a, recv_a, send_b, recv_b):
    d, t = lax.axis_index("dp"), lax.axis_index("tensor")
    beside = (d + 1 - 2 * lax.rem(d, 2), lax.rem(d + 2, 4))
    barrier = pltpu.get_barrier_semaphore()
    for o in range(1, owners):
        pl.semaphore_signal(barrier, inc=1, device_id=(d, lax.rem(t + o, owners)), device_id_type=MESH)
    for to in beside:
        pl.semaphore_signal(barrier, inc=1, device_id=(to, t), device_id_type=MESH)
    pl.semaphore_wait(barrier, owners - 1 + 2)

    def send(src, row, slot, to, kind, o):
        copy = pltpu.make_async_remote_copy(
            src_ref=src, dst_ref=out_ref.at[row, slot],
            send_sem=send_b.at[kind, o], recv_sem=recv_b.at[kind, o],
            device_id=(to, t), device_id_type=MESH)
        copy.start()
        return copy

    order = near_first(owners)
    first, direct, passed = {}, {}, []

    def outward(src, o):
        slot = lax.rem(t + owners - o, owners)
        direct[o] = [send(src, d, slot, beside[kind], kind, o) for kind in range(2)]

    def onward(i, o):
        slot = lax.rem(t + owners - o, owners)
        via = i % 2
        direct[o][via].wait_recv()
        passed.append(send(out_ref.at[beside[via], slot], beside[via], slot, beside[1 - via], 2, o))

    outward(block_ref.at[t], 0)
    for o in order:
        to = lax.rem(t + o, owners)
        first[o] = pltpu.make_async_remote_copy(
            src_ref=block_ref.at[to], dst_ref=out_ref.at[d, t],
            send_sem=send_a.at[o - 1], recv_sem=recv_a.at[o - 1],
            device_id=(d, to), device_id_type=MESH)
        first[o].start()
    own = pltpu.make_async_copy(block_ref.at[t], out_ref.at[d, t], own_sem)
    own.start()
    turns = [0] + order
    lag = 2
    for i in range(len(turns) + lag):
        if 0 < i < len(turns):
            o = turns[i]
            first[o].wait_recv()
            outward(out_ref.at[d, lax.rem(t + owners - o, owners)], o)
        if i >= lag:
            onward(i - lag, turns[i - lag])
    own.wait()
    for o in order:
        first[o].wait_send()
    for i, o in enumerate(turns):
        direct[o][1 - i % 2].wait_recv()
        direct[o][0].wait_send()
        direct[o][1].wait_send()
    for copy in passed:
        copy.wait()


def spread(blocks, n_dp):
    owners, length, side = blocks.shape
    return pl.pallas_call(
        functools.partial(square_kernel if n_dp == 4 else spread_kernel, n_dp, owners),
        out_shape=jax.ShapeDtypeStruct((n_dp, owners, length, side), blocks.dtype),
        in_specs=[pl.BlockSpec(memory_space=pl.ANY)],
        out_specs=pl.BlockSpec(memory_space=pl.ANY),
        scratch_shapes=[
            pltpu.SemaphoreType.DMA(()),
            pltpu.SemaphoreType.DMA((owners - 1,)),
            pltpu.SemaphoreType.DMA((owners - 1,)),
            pltpu.SemaphoreType.DMA((n_dp - 1, owners)),
            pltpu.SemaphoreType.DMA((n_dp - 1, owners)),
        ],
        compiler_params=pltpu.CompilerParams(collective_id=0, has_side_effects=True),
        cost_estimate=pl.CostEstimate(flops=0, bytes_accessed=2 * n_dp * blocks.size * 2, transcendentals=0),
    )(blocks)


def line_kernel(chips, chunks, part_ref, out_ref, in_ref, own_buf, mate_buf, sent, from_buf,
                own_sem, mate_send, mate_recv, line_send, line_recv):
    d, t = lax.axis_index("dp"), lax.axis_index("tensor")
    z, c = t // 2, lax.rem(t, 2)
    owners, last = 2 * chips, chips - 1
    mate = t + 1 - 2 * c
    tiles = part_ref.shape[1]
    size = tiles // chunks
    half = tiles // 2
    side = part_ref.shape[-1]
    onward = (lax.rem(t + 2, owners), lax.rem(t + owners - 2, owners))
    has_next = (z < last, z > 0)
    has_before = (z > 0, z < last)

    barrier = pltpu.get_barrier_semaphore()
    pl.semaphore_signal(barrier, inc=1, device_id=(d, mate), device_id_type=MESH)
    for way in range(2):
        @pl.when(has_next[way])
        def _():
            pl.semaphore_signal(barrier, inc=1, device_id=(d, onward[way]), device_id_type=MESH)
    inner = (z > 0) & (z < last)

    @pl.when(inner)
    def _():
        pl.semaphore_wait(barrier, 3)

    @pl.when(jnp.logical_not(inner))
    def _():
        pl.semaphore_wait(barrier, 2)

    swaps, loads = {}, {}
    order = []
    for k in range(chips // 2):
        order += [last - k, k]
    for to in order:
        swaps[to] = pltpu.make_async_remote_copy(
            src_ref=part_ref.at[2 * to + 1 - c], dst_ref=mate_buf.at[to],
            send_sem=mate_send.at[to], recv_sem=mate_recv.at[to],
            device_id=(d, mate), device_id_type=MESH)
        swaps[to].start()
        loads[to] = pltpu.make_async_copy(part_ref.at[2 * to + c], own_buf.at[to], own_sem.at[to])
        loads[to].start()

    def hop(way, to, q):
        at = pl.ds(q * size, size)
        return pltpu.make_async_remote_copy(
            src_ref=sent.at[to, at], dst_ref=from_buf.at[way, to, at],
            send_sem=line_send.at[way, to, q], recv_sem=line_recv.at[way, to, q],
            device_id=(d, onward[way]), device_id_type=MESH)

    def own_sum(to, i):
        return own_buf[to, i].astype(F32) + mate_buf[to, i].astype(F32)

    for k in range(last):
        for to in order[2 * k:2 * k + 2]:
            loads[to].wait()
            swaps[to].wait_recv()

        @pl.loop(0, chunks)
        def _(q):
            for way, to in ((0, last - k), (1, k)):
                goes = (z < to) if way == 0 else (z > to)

                @pl.when(goes & has_before[way])
                def _():
                    hop(way, to, q).wait_recv()
                    for j in range(size):
                        i = q * size + j
                        sent[to, i] = (own_sum(to, i) + from_buf[way, to, i].astype(F32)).astype(jnp.bfloat16)
                    hop(way, to, q).start()

                @pl.when(goes & jnp.logical_not(has_before[way]))
                def _():
                    for j in range(size):
                        i = q * size + j
                        sent[to, i] = own_sum(to, i).astype(jnp.bfloat16)
                    hop(way, to, q).start()

    def finish(ways):
        for q in range(chunks):
            for way in ways:
                hop(way, z, q).wait_recv()
            for j in range(size):
                i = q * size + j
                total = own_sum(z, i)
                for way in ways:
                    total = total + from_buf[way, z, i].astype(F32)
                to_ref = out_ref if i < half else in_ref
                col = i % half * side
                to_ref[:, col:col + side] = total.astype(jnp.bfloat16)

    @pl.when(z == 0)
    def _():
        finish((1,))

    @pl.when(z == last)
    def _():
        finish((0,))

    @pl.when((z > 0) & (z < last))
    def _():
        finish((0, 1))

    for to in order:
        swaps[to].wait_send()
    for k in range(last):
        @pl.loop(0, chunks)
        def _(q):
            for way, to in ((0, last - k), (1, k)):
                goes = (z < to) if way == 0 else (z > to)

                @pl.when(goes)
                def _():
                    hop(way, to, q).wait_send()


def line_sum(parts, chunks=2):
    owners, _, per, toks, side = parts.shape
    chips, tiles = owners // 2, 2 * per
    parts = parts.reshape(owners, tiles, toks, side)
    result = jax.ShapeDtypeStruct((toks, per * side), jnp.bfloat16)
    vmem = pl.BlockSpec(memory_space=pltpu.VMEM)
    return pl.pallas_call(
        functools.partial(line_kernel, chips, chunks),
        out_shape=(result, result),
        in_specs=[pl.BlockSpec(memory_space=pl.ANY)],
        out_specs=(vmem, vmem),
        scratch_shapes=[
            pltpu.VMEM((chips, tiles, toks, side), jnp.bfloat16),
            pltpu.VMEM((chips, tiles, toks, side), jnp.bfloat16),
            pltpu.VMEM((chips, tiles, toks, side), jnp.bfloat16),
            pltpu.VMEM((2, chips, tiles, toks, side), jnp.bfloat16),
            pltpu.SemaphoreType.DMA((chips,)),
            pltpu.SemaphoreType.DMA((chips,)),
            pltpu.SemaphoreType.DMA((chips,)),
            pltpu.SemaphoreType.DMA((2, chips, chunks)),
            pltpu.SemaphoreType.DMA((2, chips, chunks)),
        ],
        compiler_params=pltpu.CompilerParams(collective_id=1, has_side_effects=True, vmem_limit_bytes=58 * 2**20),
        cost_estimate=pl.CostEstimate(flops=parts.size, bytes_accessed=2 * parts.size, transcendentals=0),
    )(parts)


def tile_of(tile_ref, peer, j, g):
    side = tile_ref.shape[-1]
    at = (j % peer * 3 + g) * side
    return tile_ref[j // peer, at:at + side]


def local_kernel(dims, row_ref, col_ref, row_to_ref, col_to_ref, tok_ref, grad_ref, tile_ref, out_ref,
                 pre, back, hid, pair, acc_out, acc_in):
    rows, cols, owners, side, peer, group = dims
    phase, block = pl.program_id(0), pl.program_id(1)
    blocks = pl.num_programs(1)
    per = rows // owners

    @pl.when((phase == 0) & (block == 0))
    def _():
        @pl.loop(0, cols)
        def _(i):
            pre[i] = jnp.zeros(pre.shape[1:], F32)
            back[i] = jnp.zeros(back.shape[1:], F32)

    @pl.when(phase == 0)
    def _():
        for j in range(group):
            s = block * group + j
            at = pl.ds(pl.multiple_of(row_ref[s] * side, side), side)
            to = col_to_ref[s]
            both = jnp.concatenate([tile_of(tile_ref, peer, j, 0), tile_of(tile_ref, peer, j, 1)], axis=1)
            pre[to] += jnp.dot(tok_ref[:, at], both, preferred_element_type=F32)
            back[to] += lax.dot_general(grad_ref[:, at], tile_of(tile_ref, peer, j, 2), NT, preferred_element_type=F32)

    @pl.when((phase == 1) & (block == 0))
    def _():
        @pl.loop(0, cols)
        def _(i):
            gate = pre[i, :, :side]
            up = pre[i, :, side:]
            gh = back[i]
            s = jax.nn.sigmoid(gate)
            act = gate * s
            hid[i] = (act * up).astype(jnp.bfloat16)
            pair[i, :, :side] = (gh * up * (s * (1.0 + gate * (1.0 - s)))).astype(jnp.bfloat16)
            pair[i, :, side:] = (gh * act).astype(jnp.bfloat16)

        @pl.loop(0, rows)
        def _(i):
            acc_out[i] = jnp.zeros(acc_out.shape[1:], F32)
            acc_in[i] = jnp.zeros(acc_in.shape[1:], F32)

    @pl.when(phase == 1)
    def _():
        for j in range(group):
            s = block * group + j
            c = col_ref[s]
            to = row_to_ref[s]
            both = jnp.concatenate([tile_of(tile_ref, peer, j, 0), tile_of(tile_ref, peer, j, 1)], axis=1)
            acc_out[to] += jnp.dot(hid[c], tile_of(tile_ref, peer, j, 2), preferred_element_type=F32)
            acc_in[to] += lax.dot_general(pair[c], both, NT, preferred_element_type=F32)

    @pl.when((phase == 1) & (block == blocks - 1))
    def _():
        @pl.loop(0, owners)
        def _(k):
            for i in range(per):
                out_ref[k, 0, i] = acc_out[k * per + i].astype(jnp.bfloat16)
                out_ref[k, 1, i] = acc_in[k * per + i].astype(jnp.bfloat16)


def local_pass(tokens, out_grad, tiles, row, col, row_to, col_to, owners, cols, peer):
    toks, feats = tokens.shape
    sources, length, side = tiles.shape
    slots = sources * peer
    rows = feats // side
    whole = lambda p, b, *_: (0, 0)
    once = pl.Buffered(1)
    return pl.pallas_call(
        functools.partial(local_kernel, (rows, cols, owners, side, peer, GROUP)),
        out_shape=jax.ShapeDtypeStruct((owners, 2, rows // owners, toks, side), jnp.bfloat16),
        grid_spec=pltpu.PrefetchScalarGridSpec(
            num_scalar_prefetch=4,
            grid=(2, slots // GROUP),
            in_specs=[
                pl.BlockSpec((toks, feats), whole, pipeline_mode=once),
                pl.BlockSpec((toks, feats), whole, pipeline_mode=once),
                pl.BlockSpec((GROUP // peer, length, side), lambda p, b, *_: (b, 0, 0)),
            ],
            out_specs=pl.BlockSpec((owners, 2, rows // owners, toks, side), lambda p, b, *_: (0, 0, 0, 0, 0), pipeline_mode=once),
            scratch_shapes=[
                pltpu.VMEM((cols + 1, toks, 2 * side), F32),
                pltpu.VMEM((cols + 1, toks, side), F32),
                pltpu.VMEM((cols, toks, side), jnp.bfloat16),
                pltpu.VMEM((cols, toks, 2 * side), jnp.bfloat16),
                pltpu.VMEM((rows + 1, toks, side), F32),
                pltpu.VMEM((rows + 1, toks, side), F32),
            ],
        ),
        compiler_params=pltpu.CompilerParams(vmem_limit_bytes=58 * 2**20),
        cost_estimate=pl.CostEstimate(flops=12 * slots * toks * side * side, bytes_accessed=30 * 2**20, transcendentals=0),
    )(row, col, row_to, col_to, tokens, out_grad, tiles)


def body(tokens, out_grad, weight_tiles, tile_places, live_counts):
    toks, feats = tokens.shape
    side = weight_tiles.shape[-1]
    peer = weight_tiles.shape[1]
    rows = feats // side
    owners = lax.axis_size("tensor")
    cols = FF // (side * owners)
    n_dp = lax.axis_size("dp")
    live = jnp.arange(peer)[None, :] < live_counts[:, None]
    meta = jnp.concatenate([tile_places // cols, tile_places % cols, live.astype(jnp.int32)], axis=1)
    meta = jnp.pad(meta.astype(jnp.bfloat16), ((0, 0), (0, side - 3 * peer)))
    meta = jnp.broadcast_to(meta[:, None, :], (owners, META, side))
    blocks = jnp.concatenate([weight_tiles.reshape(owners, -1, side), meta], axis=1)
    tiles = spread(blocks, n_dp)
    tiles = tiles.reshape((n_dp * owners,) + tiles.shape[2:])
    meta = tiles[:, -META, :3 * peer].astype(jnp.int32)
    row = meta[:, :peer].reshape(-1)
    col = meta[:, peer:2 * peer].reshape(-1)
    live = meta[:, 2 * peer:].reshape(-1) > 0
    row_to = jnp.where(live, row, rows)
    col_to = jnp.where(live, col, cols)
    parts = local_pass(tokens, out_grad, tiles, row, col, row_to, col_to, owners, cols, peer)
    if (n_dp, owners) == (4, 8):
        return line_sum(parts)
    total = lax.psum_scatter(parts, "tensor", scatter_dimension=0, tiled=True)
    total = jnp.transpose(total[0], (0, 2, 1, 3)).reshape(2, toks, feats // owners)
    return total[0], total[1]


def solution(mesh):
    in_specs = (
        P("dp", None),
        P("dp", None),
        P(("dp", "tensor"), None, None, None, None),
        P(("dp", "tensor"), None),
        P(("dp", "tensor")),
    )
    out_specs = (P("dp", "tensor"), P("dp", "tensor"))
    return jax.shard_map(body, mesh=mesh, in_specs=in_specs, out_specs=out_specs, check_vma=False)
```
